32 devices in a mesh: strip: 4 (over x, core), blk: 8 (over z, y).
Axes of the slice: x: 2, y: 2, z: 4, core: 2. Of those that a mesh axis runs over, the one named last changes fastest.
Arguments:
- objects: float32 [2, 2, 512, 1024], P(None, None, 'strip', 'blk'), may hold values from 0.5 to 1
- probe_init: float32 [2, 64, 256], replicated, may hold values from -1 to 1
- scan_rows: int32 [64], P(('strip', 'blk')), may hold values from 0 to 64
- scan_cols: int32 [64], P(('strip', 'blk')), may hold values from 0 to 64
- amplitudes: float32 [64, 4096], P(('strip', 'blk')), may hold values from 0.5 to 2.5
- counts: int32 [32], P(('strip', 'blk')), may hold values from 1 to 2, 48 in all
- offsets: int32 [4], replicated, may hold values from 0 to 127
Outputs:
- refined_object: float32 [2, 2, 512, 1024], P(None, None, 'strip', 'blk')
- probe_step: float32 [2, 64, 256], P(None, None, 'blk')
The draws below stay inside these ranges and needn't reach their ends.
Inputs may be any that keep to these rules, and one draw needn't show every extreme that they name: `counts`: A device's slots from its count on are unused. `offsets`: the last entry is unused.
All inputs are finite; a program needn't handle non-finite values.
Results may differ from the reference program's by a relative error of at most 0.0001.
Values sent between devices are 32-bit elements; how exact they have to be, the bound alone decides.
A program may use at most 64 MiB of HBM per device.

```python
import math
import jax
import jax.numpy as jnp
import numpy as np
from jax import lax

W = 64
M = 4
NS = 2
ROUNDS = 2
BORDER = 32
CAP = 2
TX = 128
TY = 128
NX = 512
NY = 1024
SLOTS = 64
N_STRIP = 4
N_BLK = 8


def with_ends(array, key, smallest, high):
    shape = array.shape
    spot = [jax.random.randint(jax.random.fold_in(key, axis), (), 0, shape[axis]) for axis in range(len(shape))]
    array = array.at[tuple(spot)].set(smallest)
    longest = shape.index(max(shape))
    spot[longest] = (spot[longest] + 1) % shape[longest]
    return array.at[tuple(spot)].set(high)


def block_levels(key, dims, split, smallest, top_value):
    factor_of, own = 1.0, jax.random.fold_in(key, 6)
    for dim, blocks in split:
        steps = jnp.exp(jax.random.uniform(jax.random.fold_in(own, dim), (blocks,), jnp.float32, smallest / len(split), top_value / len(split)))
        factor_of = factor_of * jnp.repeat(steps, dims[dim] // blocks).reshape([-1 if axis == dim else 1 for axis in range(len(dims))])
    return factor_of


def split_up(amount, total, limit, lean):
    weights = [(1 << 20) // math.isqrt(standing ** lean) + 1 for standing in range(2, amount + 1)]
    surplus, given = total - limit - (amount - 1), [1] * (amount - 1)
    while surplus > 0:
        free = [i for i in range(amount - 1) if given[i] < limit]
        pool, left = sum([weights[i] for i in free]), surplus
        for i in free:
            extra = min(limit - given[i], max(1, left * weights[i] // pool), surplus)
            given[i] = given[i] + extra
            surplus = surplus - extra
    return np.array([limit] + given)


def uneven(stream_key, count, total, reach, lean):
    if count == 2:
        one = jax.random.randint(stream_key, (), max(1, total - reach), min(reach, total - 1) + 1)
        return jnp.stack([one, total - one])
    tallies = jnp.asarray(split_up(count, total, reach, lean), jnp.int32)
    twos = (count - 1) // 2
    donor, sink = tallies[1:1 + 2 * twos:2], tallies[2:2 + 2 * twos:2]
    margin = jnp.minimum(donor - 1, reach - sink)
    passed = jax.random.randint(jax.random.fold_in(stream_key, 1), (twos,), 0, 1 << 20) % (margin + 1)
    tallies = tallies.at[1:1 + 2 * twos:2].set(donor - passed).at[2:2 + 2 * twos:2].set(sink + passed)
    return tallies[jax.random.permutation(jax.random.fold_in(stream_key, 2), count)]


def setup_inputs(seed: int = 0) -> dict:
    key_of = jax.random.split(jax.random.key(seed), 8)
    objects = jnp.clip(0.5 + 0.5 * jax.random.uniform(key_of[0], (2, NS, NX, NY), jnp.float32) ** block_levels(key_of[0], (2, NS, NX, NY), ((2, 4), (3, 8)), -0.2, 0.2), 0.5, 1.0)
    probe_init = jnp.clip(jax.random.uniform(key_of[1], (2, W, M * W), jnp.float32, -1.0, 1.0), -1.0, 1.0)
    scan_rows = with_ends(jax.random.randint(key_of[2], (SLOTS,), 0, TX - W + 1), jax.random.fold_in(key_of[2], 1), 0, TX - W).astype(jnp.int32)
    scan_cols = with_ends(jax.random.randint(key_of[3], (SLOTS,), 0, TY - W + 1), jax.random.fold_in(key_of[3], 1), 0, TY - W).astype(jnp.int32)
    amplitudes = jnp.clip(0.5 + 2.0 * jax.random.uniform(key_of[4], (SLOTS, W * W), jnp.float32) ** block_levels(key_of[4], (SLOTS, W * W), ((0, 32),), -0.2, 0.2), 0.5, 2.5)
    counts = uneven(key_of[5], N_STRIP * N_BLK, N_STRIP * N_BLK * CAP * 3 // 4, CAP, 1).astype(jnp.int32)
    offsets = with_ends(jax.random.randint(key_of[6], (N_STRIP,), 0, TY), jax.random.fold_in(key_of[6], 1), 0, TY - 1).astype(jnp.int32)
    return dict(objects=objects, probe_init=probe_init, scan_rows=scan_rows, scan_cols=scan_cols, amplitudes=amplitudes, counts=counts, offsets=offsets)


full_precision = lax.Precision.HIGHEST
object_rate = 0.3
probe_rate = 0.5
modulus_floor = 0.25
fresnel_phase = 0.15
power_epsilon = 1e-06

def dft_tables(window):
    position = jnp.arange(window, dtype=jnp.int32)
    product = position[:, None] * position[None, :] % window
    phase_angle = product.astype(jnp.float32) * (2.0 * jnp.pi / window)
    norm_scale = 1.0 / jnp.sqrt(jnp.float32(window))
    return (jnp.cos(phase_angle) * norm_scale, -jnp.sin(phase_angle) * norm_scale)

def fresnel_kernel(window):
    position = jnp.arange(window, dtype=jnp.int32)
    frequency = jnp.where(position < window // 2, position, position - window)
    square = (frequency[:, None] ** 2 + frequency[None, :] ** 2).astype(jnp.float32)
    phase_grid = square * (fresnel_phase / window)
    return (jnp.cos(phase_grid), jnp.sin(phase_grid))

def left_apply(table_re, table_im, part_re, part_im):

    def single(table_part, data_part):
        return jnp.einsum('kn,qnc->qkc', table_part, data_part, precision=full_precision)
    return (single(table_re, part_re) - single(table_im, part_im), single(table_re, part_im) + single(table_im, part_re))

def right_apply(part_re, part_im, table_re, table_im):

    def single(data_part, table_part):
        return jnp.einsum('qrn,nc->qrc', data_part, table_part, precision=full_precision)
    return (single(part_re, table_re) - single(part_im, table_im), single(part_re, table_im) + single(part_im, table_re))

def transform(complex_pair, tables, inverse):
    cos_table, sin_table = tables
    if inverse:
        sin_table = -sin_table
    middle = left_apply(cos_table, sin_table, complex_pair[0], complex_pair[1])
    return right_apply(middle[0], middle[1], cos_table, sin_table)

def complex_times(left_pair, right_pair):
    return (left_pair[0] * right_pair[0] - left_pair[1] * right_pair[1], left_pair[0] * right_pair[1] + left_pair[1] * right_pair[0])

def conjugate_times(left_pair, right_pair):
    return (left_pair[0] * right_pair[0] + left_pair[1] * right_pair[1], left_pair[0] * right_pair[1] - left_pair[1] * right_pair[0])

def round_update(tile_data, probe_now, row_starts, col_starts, amplitudes, weights, tables, kernel):
    window = probe_now.shape[1]
    mode_count = probe_now.shape[2] // window
    slot_count = row_starts.shape[0]
    layers = tile_data.shape[1]
    anchor = jnp.zeros((), jnp.int32)
    probe_modes = probe_now.reshape(2, window, mode_count, window).transpose(0, 2, 1, 3)

    def window_of(row_start, col_start):
        return lax.dynamic_slice(tile_data, (anchor, anchor, row_start, col_start), (2, layers, window, window))
    windows = jax.vmap(window_of)(row_starts, col_starts)
    first_obj = (windows[:, 0, 0][:, None], windows[:, 1, 0][:, None])
    second_obj = (windows[:, 0, 1][:, None], windows[:, 1, 1][:, None])
    probe_pair = (probe_modes[0][None], probe_modes[1][None])

    def flatten(complex_pair):
        return (complex_pair[0].reshape(slot_count * mode_count, window, window), complex_pair[1].reshape(slot_count * mode_count, window, window))

    def unflatten(complex_pair):
        return (complex_pair[0].reshape(slot_count, mode_count, window, window), complex_pair[1].reshape(slot_count, mode_count, window, window))
    entrance = complex_times(probe_pair, first_obj)
    spectrum = complex_times(transform(flatten(entrance), tables, False), kernel)
    arrival = unflatten(transform(spectrum, tables, True))
    departure = complex_times(arrival, second_obj)
    farfield = unflatten(transform(flatten(departure), tables, False))
    modulus = jnp.sqrt(lax.optimization_barrier(jnp.sum(farfield[0] ** 2 + farfield[1] ** 2, axis=1)))
    measured = amplitudes.reshape(slot_count, window, window)
    factor = (measured / jnp.maximum(modulus, modulus_floor) - 1.0) * weights[:, None, None]
    change = (farfield[0] * factor[:, None], farfield[1] * factor[:, None])
    exit_change = unflatten(transform(flatten(change), tables, True))
    second_terms = conjugate_times(arrival, exit_change)
    second_update = (lax.optimization_barrier(jnp.sum(second_terms[0], axis=1)), lax.optimization_barrier(jnp.sum(second_terms[1], axis=1)))
    arrival_change = conjugate_times(second_obj, exit_change)
    back_spectrum = conjugate_times(kernel, transform(flatten(arrival_change), tables, False))
    entrance_change = unflatten(transform(back_spectrum, tables, True))
    first_terms = conjugate_times(probe_pair, entrance_change)
    first_update = (lax.optimization_barrier(jnp.sum(first_terms[0], axis=1)), lax.optimization_barrier(jnp.sum(first_terms[1], axis=1)))
    probe_terms = conjugate_times(first_obj, entrance_change)
    probe_change = (lax.optimization_barrier(jnp.sum(probe_terms[0], axis=0)), lax.optimization_barrier(jnp.sum(probe_terms[1], axis=0)))
    tile_pixels = tile_data.shape[2] * tile_data.shape[3]
    probe_power = jnp.sum(probe_now * probe_now) / (window * window) + power_epsilon
    first_power = jnp.sum(tile_data[:, 0] * tile_data[:, 0]) / tile_pixels + power_epsilon
    second_power = jnp.sum(tile_data[:, 1] * tile_data[:, 1]) / tile_pixels + power_epsilon
    probe_gain = probe_rate / (first_power * second_power * slot_count)
    new_modes = jnp.stack([probe_modes[0] + probe_gain * probe_change[0], probe_modes[1] + probe_gain * probe_change[1]])
    new_probe = new_modes.transpose(0, 2, 1, 3).reshape(2, window, mode_count * window)
    first_gain = object_rate / (probe_power * slot_count)
    second_gain = object_rate / (probe_power * first_power * slot_count)
    first_stack = jnp.stack([first_update[0], first_update[1]], axis=1) * first_gain
    second_stack = jnp.stack([second_update[0], second_update[1]], axis=1) * second_gain
    updates = jnp.stack([first_stack, second_stack], axis=2)

    def place_update(slot_index, current):
        corner = (anchor, anchor, row_starts[slot_index], col_starts[slot_index])
        old_block = lax.dynamic_slice(current, corner, (2, layers, window, window))
        return lax.dynamic_update_slice(current, old_block + updates[slot_index], corner)
    new_tile = lax.fori_loop(0, slot_count, place_update, tile_data)
    return (new_tile, new_probe)

def average_borders(objects, offsets):
    layers = objects.shape[1]
    pixel_grid = objects.reshape(2, layers, N_STRIP, TX, NY)
    lower_rows = pixel_grid[:, :, :-1, TX - BORDER:, :]
    upper_rows = pixel_grid[:, :, 1:, :BORDER, :]
    col_shift = offsets[:-1].astype(jnp.int32)
    column = jnp.arange(NY, dtype=jnp.int32)
    ahead_col = column[None, :] + col_shift[:, None]
    behind_col = column[None, :] - col_shift[:, None]
    full_shape = lower_rows.shape
    ahead_index = jnp.broadcast_to(jnp.clip(ahead_col, 0, NY - 1)[None, None, :, None, :], full_shape)
    behind_index = jnp.broadcast_to(jnp.clip(behind_col, 0, NY - 1)[None, None, :, None, :], full_shape)
    upper_ahead = jnp.take_along_axis(upper_rows, ahead_index, axis=4)
    lower_behind = jnp.take_along_axis(lower_rows, behind_index, axis=4)
    keep_ahead = (ahead_col < NY)[None, None, :, None, :]
    keep_behind = (behind_col >= 0)[None, None, :, None, :]
    new_lower = jnp.where(keep_ahead, 0.5 * (lower_rows + upper_ahead), lower_rows)
    new_upper = jnp.where(keep_behind, 0.5 * (upper_rows + lower_behind), upper_rows)
    pixel_grid = pixel_grid.at[:, :, :-1, TX - BORDER:, :].set(new_lower)
    pixel_grid = pixel_grid.at[:, :, 1:, :BORDER, :].set(new_upper)
    return pixel_grid.reshape(objects.shape)

def reference(objects, probe_init, scan_rows, scan_cols, amplitudes, counts, offsets):
    devices = N_STRIP * N_BLK
    layers = objects.shape[1]
    tile_set = objects.reshape(2, layers, N_STRIP, TX, N_BLK, TY).transpose(2, 4, 0, 1, 3, 5)
    tile_set = tile_set.reshape(devices, 2, layers, TX, TY)
    row_starts = scan_rows.reshape(devices, CAP)
    col_starts = scan_cols.reshape(devices, CAP)
    measured = amplitudes.reshape(devices, CAP, W * W)
    weights = (jnp.arange(CAP, dtype=jnp.int32)[None, :] < counts[:, None]).astype(jnp.float32)
    probes = jnp.broadcast_to(probe_init[None], (devices,) + probe_init.shape)
    tables = dft_tables(W)
    kernel = fresnel_kernel(W)

    def device_round(device_items):
        return round_update(device_items[0], device_items[1], device_items[2], device_items[3], device_items[4], device_items[5], tables, kernel)
    for round_index in range(ROUNDS):
        if round_index > 0:
            probes = jnp.roll(probes.reshape((N_STRIP, N_BLK) + probe_init.shape), 1, axis=1)
            probes = probes.reshape((devices,) + probe_init.shape)
        tile_set, probes = lax.map(device_round, (tile_set, probes, row_starts, col_starts, measured, weights))
    probe_step = lax.optimization_barrier(jnp.sum(probes - probe_init[None], axis=0)) / (N_STRIP * N_BLK)
    merged = tile_set.reshape(N_STRIP, N_BLK, 2, layers, TX, TY).transpose(2, 3, 0, 4, 1, 5)
    merged = merged.reshape(objects.shape)
    return (average_borders(merged, offsets), probe_step)
```

```python
import functools

import jax
import jax.numpy as jnp
import ml_dtypes
import numpy as np
from jax import lax
from jax.experimental import pallas as pl
from jax.experimental.pallas import tpu as pltpu
from jax.sharding import PartitionSpec as P

ROUNDS = 2
BORDER = 32
object_rate = 0.3
probe_rate = 0.5
modulus_floor = 0.25
fresnel_phase = 0.15
power_epsilon = 1e-06
MESH = pl.DeviceIdType.MESH


def two_parts(table):
    high = table.astype(ml_dtypes.bfloat16)
    low = (table - high.astype(np.float64)).astype(ml_dtypes.bfloat16)
    return [high, low]


def tables_of(window, modes):
    position = np.arange(window)
    angle = (position[:, None] * position[None, :] % window) * (2 * np.pi / window)
    dft = (np.cos(angle) - 1j * np.sin(angle)) / np.sqrt(window)
    frequency = np.where(position < window // 2, position, position - window)
    phase = np.exp(1j * fresnel_phase * frequency.astype(np.float64) ** 2 / window)
    fresnel = np.conj(dft) @ (phase[:, None] * dft)
    left, right = [], []
    for matrix in (dft, np.conj(dft), fresnel, np.conj(fresnel)):
        left += two_parts(np.block([[matrix.real, -matrix.imag], [matrix.imag, matrix.real]]))
    for matrix in (dft, fresnel):
        for part in (matrix.real, matrix.imag):
            right += two_parts(np.kron(np.eye(modes), part))
    return np.stack(left), np.stack(right)


def halves(value):
    high = value.astype(jnp.bfloat16)
    return high, (value - high.astype(jnp.float32)).astype(jnp.bfloat16)


def product(left, right):
    return jnp.dot(left, right, preferred_element_type=jnp.float32)


def kernel(
    n_strip, n_blk,
    rows_ref, cols_ref, counts_ref, offsets_ref,
    objects_ref, probe_ref, amps_ref, left_ref, right_ref,
    out_ref, step_ref,
    tile, spread, probe_out, probe_in,
    shares, arrived, partial, strips, rims,
    ring_sems, share_send, share_recv, strip_send, strip_recv, rim_send, rim_recv,
):
    s, b = lax.axis_index("strip"), lax.axis_index("blk")
    window, width = probe_ref.shape[1], probe_ref.shape[2]
    modes = width // window
    slots = amps_ref.shape[0]
    size = objects_ref.shape[2]
    share = shares.shape[1]
    groups = 128 // share

    def blk_step(k):
        return lax.rem(b + k + n_blk, n_blk)

    def strip_step(k):
        return lax.rem(s + k + n_strip, n_strip)

    rims[...] = jnp.zeros_like(rims)
    barrier = pltpu.get_barrier_semaphore()
    partners = [(s, blk_step(k)) for k in range(1, n_blk)]
    partners += [(strip_step(k), b) for k in range(1, n_strip)]
    partners += [(strip_step(k), blk_step(k)) for k in (-1, 1)]
    for partner in partners:
        pl.semaphore_signal(barrier, inc=1, device_id=partner, device_id_type=MESH)

    def transform(pairs, left_index, right_index, sign):
        left_high, left_low = left_ref[left_index], left_ref[left_index + 1]
        middles = []
        for re, im in pairs:
            high, low = halves(jnp.concatenate([re, im], axis=0))
            middles.append(product(left_high, high) + product(left_high, low) + product(left_low, high))
        high, low = halves(jnp.concatenate(middles, axis=0))
        sums = []
        for index in (right_index, right_index + 2):
            table_high, table_low = right_ref[index], right_ref[index + 1]
            sums.append(product(high, table_high) + product(high, table_low) + product(low, table_high))
        by_re, by_im = sums
        results = []
        for j in range(len(pairs)):
            re_rows = slice(2 * j * window, (2 * j + 1) * window)
            im_rows = slice((2 * j + 1) * window, (2 * j + 2) * window)
            if sign > 0:
                results.append((by_re[re_rows] - by_im[im_rows], by_im[re_rows] + by_re[im_rows]))
            else:
                results.append((by_re[re_rows] + by_im[im_rows], by_re[im_rows] - by_im[re_rows]))
        return results

    def times(x, y):
        return x[0] * y[0] - x[1] * y[1], x[0] * y[1] + x[1] * y[0]

    def conj_times(x, y):
        return x[0] * y[0] + x[1] * y[1], x[0] * y[1] - x[1] * y[0]

    lane = lax.broadcasted_iota(jnp.int32, (window, 128), 1)

    def over_modes(value):
        total = value[:, :128]
        for start in range(128, width, 128):
            total = total + value[:, start : start + 128]
        return total + pltpu.roll(total, window, 1)

    def widened(value):
        return jnp.concatenate([value] * (width // 128), axis=1)

    def window_of(source, part, layer, j):
        rows = source[part, layer, pl.ds(rows_ref[j], window), :]
        rows = pltpu.roll(rows, lax.rem(size - cols_ref[j], size), 1)
        return widened(jnp.where(lane < window, rows, pltpu.roll(rows, window, 1)))

    def total_of(value):
        return jnp.sum(jnp.sum(value, axis=0, keepdims=True), axis=1, keepdims=True)

    spread[...] = jnp.zeros_like(spread)

    def placed(buffer, value, j):
        spread[buffer, pl.ds(size - window, window), :] = jnp.where(lane < window, value, 0.0)
        rows = spread[buffer, pl.ds(size - window - rows_ref[j], size), :]
        return pltpu.roll(rows, cols_ref[j], 1)

    rim_rows = (pl.ds(0, BORDER), pl.ds(size - BORDER, BORDER))
    rim_plan = (
        (0, -1, 0, s > 0, s < n_strip - 1),
        (0, -1, -1, (s > 0) & (b > 0), (s < n_strip - 1) & (b < n_blk - 1)),
        (1, 1, 0, s < n_strip - 1, s > 0),
        (1, 1, 1, (s < n_strip - 1) & (b < n_blk - 1), (s > 0) & (b > 0)),
    )

    def rim_copy(layer, kind):
        edge, ds, db, _, _ = rim_plan[kind]
        return pltpu.make_async_remote_copy(
            src_ref=tile.at[:, layer, rim_rows[edge], :],
            dst_ref=rims.at[kind, layer],
            send_sem=rim_send.at[kind, layer],
            recv_sem=rim_recv.at[kind, layer],
            device_id=(strip_step(ds), blk_step(db)),
            device_id_type=MESH,
        )

    def send_rims(layer):
        for kind in range(4):
            @pl.when(rim_plan[kind][3])
            def _():
                rim_copy(layer, kind).start()

    ring = pltpu.make_async_remote_copy(
        src_ref=probe_out, dst_ref=probe_in,
        send_sem=ring_sems.at[0], recv_sem=ring_sems.at[1],
        device_id=(s, blk_step(1)), device_id_type=MESH,
    )

    for round_index in range(ROUNDS):
        last = round_index == ROUNDS - 1
        source = objects_ref if round_index == 0 else tile
        probe_src = probe_ref if round_index == 0 else probe_in
        powers = []
        for layer in range(2):
            squares = source[0, layer] ** 2 + source[1, layer] ** 2
            powers.append(total_of(squares) / (size * size) + power_epsilon)
        objects = [
            [(window_of(source, 0, layer, j), window_of(source, 1, layer, j)) for j in range(slots)]
            for layer in range(2)
        ]
        if round_index > 0:
            ring.wait_recv()
        probe = (probe_src[0], probe_src[1])
        probe_power = total_of(probe[0] ** 2 + probe[1] ** 2) / (window * window) + power_epsilon
        arrivals = transform([times(probe, objects[0][j]) for j in range(slots)], 4, 4, 1)
        far = transform([times(arrivals[j], objects[1][j]) for j in range(slots)], 0, 0, 1)
        changes = []
        for j in range(slots):
            weight = jnp.where(counts_ref[0] > j, 1.0, 0.0)
            modulus = jnp.sqrt(over_modes(far[j][0] ** 2 + far[j][1] ** 2))
            amps = jnp.concatenate([amps_ref[j]] * (128 // window), axis=1)
            factor = widened((amps / jnp.maximum(modulus, modulus_floor) - 1.0) * weight)
            changes.append((far[j][0] * factor, far[j][1] * factor))
        exits = transform(changes, 2, 0, -1)

        second_gain = object_rate / (probe_power * powers[0] * slots)
        for part in range(2):
            total = source[part, 1]
            for j in range(slots):
                update = over_modes(conj_times(arrivals[j], exits[j])[part]) * second_gain
                total = total + placed(2 * j + part, update, j)
            tile[part, 1] = total
        if last:
            send_rims(1)

        entries = transform([conj_times(objects[1][j], exits[j]) for j in range(slots)], 6, 4, -1)
        probe_gain = probe_rate / (powers[0] * powers[1] * slots)
        terms = [conj_times(objects[0][j], entries[j]) for j in range(slots)]
        moved = []
        for part in range(2):
            total = terms[0][part]
            for j in range(1, slots):
                total = total + terms[j][part]
            moved.append(probe[part] + probe_gain * total)
        if not last:
            for part in range(2):
                probe_out[part] = moved[part]
            if round_index == 0:
                pl.semaphore_wait(barrier, len(partners))
            ring.start()
        else:
            stacked = jnp.concatenate([moved[0] - probe_ref[0], moved[1] - probe_ref[1]], axis=0)
            group_of = lax.broadcasted_iota(jnp.int32, (share, 128), 1) // share
            for h in range(width // 128):
                for i in range(groups):
                    packed = None
                    for k in range(groups):
                        block = stacked[k * share : (k + 1) * share, h * 128 : (h + 1) * 128]
                        if k != i:
                            block = pltpu.roll(block, (k - i) % groups * share, 1)
                        packed = block if packed is None else jnp.where(group_of == k, block, packed)
                    shares[h * groups + i] = packed
            share_copies = []
            for k in range(1, n_blk):
                share_copies.append(
                    pltpu.make_async_remote_copy(
                        src_ref=shares.at[blk_step(k)], dst_ref=arrived.at[k],
                        send_sem=share_send.at[k], recv_sem=share_recv.at[k],
                        device_id=(s, blk_step(k)), device_id_type=MESH,
                    )
                )
                share_copies[-1].start()

        first_gain = object_rate / (probe_power * slots)
        for part in range(2):
            total = source[part, 0]
            for j in range(slots):
                update = over_modes(conj_times(probe, entries[j])[part]) * first_gain
                total = total + placed(2 * j + part, update, j)
            tile[part, 0] = total
        if last:
            send_rims(0)
        else:
            ring.wait_send()

    own = shares[b]
    for k in range(1, n_blk):
        share_copies[k - 1].wait_recv()
        own = own + arrived[k]
    partial[...] = own
    strip_copies = []
    for k in range(1, n_strip):
        strip_copies.append(
            pltpu.make_async_remote_copy(
                src_ref=partial, dst_ref=strips.at[k],
                send_sem=strip_send.at[k], recv_sem=strip_recv.at[k],
                device_id=(strip_step(k), b), device_id_type=MESH,
            )
        )
        strip_copies[-1].start()

    for part in range(2):
        for layer in range(2):
            out_ref[part, layer, pl.ds(BORDER, size - 2 * BORDER), :] = tile[
                part, layer, pl.ds(BORDER, size - 2 * BORDER), :
            ]
    for layer in (1, 0):
        for kind in range(4):
            @pl.when(rim_plan[kind][4])
            def _():
                rim_copy(layer, kind).wait_recv()
    column = lax.broadcasted_iota(jnp.int32, (BORDER, size), 1)
    down = offsets_ref[s]
    up = offsets_ref[jnp.maximum(s - 1, 0)]
    for layer in range(2):
        for part in range(2):
            partner = pltpu.roll(
                jnp.where(column >= down, rims[0, layer, part], rims[1, layer, part]),
                lax.rem(size - down, size), 1,
            )
            valid = (s < n_strip - 1) & ((b < n_blk - 1) | (column + down < size))
            mine = tile[part, layer, rim_rows[1], :]
            out_ref[part, layer, rim_rows[1], :] = jnp.where(valid, 0.5 * (mine + partner), mine)
            partner = pltpu.roll(
                jnp.where(column < size - up, rims[2, layer, part], rims[3, layer, part]), up, 1
            )
            valid = (s > 0) & ((b > 0) | (column >= up))
            mine = tile[part, layer, rim_rows[0], :]
            out_ref[part, layer, rim_rows[0], :] = jnp.where(valid, 0.5 * (mine + partner), mine)

    total = partial[...]
    for k in range(1, n_strip):
        strip_copies[k - 1].wait_recv()
        total = total + strips[k]
    total = total / (n_strip * n_blk)
    for k in range(groups):
        block = total if k == 0 else pltpu.roll(total, (groups - k) * share, 1)
        part, row = divmod(k * share, window)
        step_ref[part, pl.ds(row, share), :] = block[:, :share]

    for copy in share_copies + strip_copies:
        copy.wait_send()
    for layer in range(2):
        for kind in range(4):
            @pl.when(rim_plan[kind][3])
            def _():
                rim_copy(layer, kind).wait_send()


def shards(n_strip, n_blk, objects, probe_init, scan_rows, scan_cols, amplitudes, counts, offsets):
    window, width = probe_init.shape[1], probe_init.shape[2]
    slots = scan_rows.shape[0]
    size = objects.shape[2]
    share = width // n_blk
    left, right = tables_of(window, width // window)
    smem = pl.BlockSpec(memory_space=pltpu.SMEM)
    vmem = pl.BlockSpec(memory_space=pltpu.VMEM)
    dma = pltpu.SemaphoreType.DMA
    return pl.pallas_call(
        functools.partial(kernel, n_strip, n_blk),
        out_shape=(
            jax.ShapeDtypeStruct(objects.shape, jnp.float32),
            jax.ShapeDtypeStruct((2, window, share), jnp.float32),
        ),
        in_specs=[smem] * 4 + [vmem] * 5,
        out_specs=(vmem, vmem),
        scratch_shapes=[
            pltpu.VMEM(objects.shape, jnp.float32),
            pltpu.VMEM((2 * slots, 2 * size - window, size), jnp.float32),
            pltpu.VMEM(probe_init.shape, jnp.float32),
            pltpu.VMEM(probe_init.shape, jnp.float32),
            pltpu.VMEM((n_blk, share, 128), jnp.float32),
            pltpu.VMEM((n_blk, share, 128), jnp.float32),
            pltpu.VMEM((share, 128), jnp.float32),
            pltpu.VMEM((n_strip, share, 128), jnp.float32),
            pltpu.VMEM((4, 2, 2, BORDER, size), jnp.float32),
            dma((2,)),
            dma((n_blk,)), dma((n_blk,)),
            dma((n_strip,)), dma((n_strip,)),
            dma((4, 2)), dma((4, 2)),
        ],
        compiler_params=pltpu.CompilerParams(
            collective_id=0, has_side_effects=True, vmem_limit_bytes=40 * 1024 * 1024
        ),
    )(
        scan_rows, scan_cols, counts, offsets,
        objects, probe_init, amplitudes.reshape(slots, window, window),
        jnp.asarray(left), jnp.asarray(right),
    )


def solution(mesh):
    return jax.shard_map(
        functools.partial(shards, mesh.shape["strip"], mesh.shape["blk"]),
        mesh=mesh,
        in_specs=(
            P(None, None, "strip", "blk"),
            P(),
            P(("strip", "blk")),
            P(("strip", "blk")),
            P(("strip", "blk"), None),
            P(("strip", "blk")),
            P(),
        ),
        out_specs=(P(None, None, "strip", "blk"), P(None, None, "blk")),
        check_vma=False,
    )
```

```python
import functools

import jax
import jax.numpy as jnp
import ml_dtypes
import numpy as np
from jax import lax
from jax.experimental import pallas as pl
from jax.experimental.pallas import tpu as pltpu
from jax.sharding import PartitionSpec as P

ROUNDS = 2
BORDER = 32
object_rate = 0.3
probe_rate = 0.5
modulus_floor = 0.25
fresnel_phase = 0.15
power_epsilon = 1e-06
MESH = pl.DeviceIdType.MESH


def two_parts(table):
    high = table.astype(ml_dtypes.bfloat16)
    low = (table - high.astype(np.float64)).astype(ml_dtypes.bfloat16)
    return [high, low]


def tables_of(window, modes):
    position = np.arange(window)
    angle = (position[:, None] * position[None, :] % window) * (2 * np.pi / window)
    dft = (np.cos(angle) - 1j * np.sin(angle)) / np.sqrt(window)
    frequency = np.where(position < window // 2, position, position - window)
    phase = np.exp(1j * fresnel_phase * frequency.astype(np.float64) ** 2 / window)
    fresnel = np.conj(dft) @ (phase[:, None] * dft)
    left, right = [], []
    for matrix in (dft, np.conj(dft), fresnel, np.conj(fresnel)):
        left += two_parts(np.block([[matrix.real, -matrix.imag], [matrix.imag, matrix.real]]))
    for matrix in (dft, fresnel):
        for part in (matrix.real, matrix.imag):
            right += two_parts(np.kron(np.eye(modes), part))
    return np.stack(left), np.stack(right)


def halves(value):
    high = value.astype(jnp.bfloat16)
    return high, (value - high.astype(jnp.float32)).astype(jnp.bfloat16)


def product(left, right):
    return jnp.dot(left, right, preferred_element_type=jnp.float32)


def kernel(
    n_strip, n_blk,
    rows_ref, cols_ref, counts_ref, offsets_ref,
    objects_hbm, probe_hbm, amps_hbm, left_hbm, right_hbm,
    out_ref, step_ref,
    objects_ref, probe_ref, amps_raw, left_ref, right_ref, amps_ref, in_sems,
    tile, spread, probe_out, probe_in,
    shares, arrived, partial, strips, rims,
    ring_sems, share_send, share_recv, strip_send, strip_recv, rim_send, rim_recv,
):
    s, b = lax.axis_index("strip"), lax.axis_index("blk")
    window, width = probe_ref.shape[1], probe_ref.shape[2]
    modes = width // window
    slots = amps_ref.shape[0]
    size = objects_ref.shape[2]
    both = pl.ds(0, 4), pl.ds(4, 4)
    loads = [
        pltpu.make_async_copy(source, target, in_sems.at[i])
        for i, (source, target) in enumerate((
            (objects_hbm, objects_ref),
            (probe_hbm, probe_ref),
            (left_hbm.at[both[1]], left_ref.at[both[1]]),
            (right_hbm.at[both[1]], right_ref.at[both[1]]),
            (left_hbm.at[both[0]], left_ref.at[both[0]]),
            (right_hbm.at[both[0]], right_ref.at[both[0]]),
            (amps_hbm, amps_raw),
        ))
    ]
    for load in loads:
        load.start()
    share = shares.shape[1]
    groups = 128 // share

    def blk_step(k):
        return lax.rem(b + k + n_blk, n_blk)

    def strip_step(k):
        return lax.rem(s + k + n_strip, n_strip)

    rims[...] = jnp.zeros_like(rims)
    barrier = pltpu.get_barrier_semaphore()
    partners = [(s, blk_step(k)) for k in range(1, n_blk)]
    partners += [(strip_step(k), b) for k in range(1, n_strip)]
    partners += [(strip_step(k), blk_step(k)) for k in (-1, 1)]
    for partner in partners:
        pl.semaphore_signal(barrier, inc=1, device_id=partner, device_id_type=MESH)

    def transform(pairs, left_index, right_index, sign):
        left_high, left_low = left_ref[left_index], left_ref[left_index + 1]
        middles = []
        for re, im in pairs:
            high, low = halves(jnp.concatenate([re, im], axis=0))
            middles.append(product(left_high, high) + product(left_high, low) + product(left_low, high))
        high, low = halves(jnp.concatenate(middles, axis=0))
        sums = []
        for index in (right_index, right_index + 2):
            table_high, table_low = right_ref[index], right_ref[index + 1]
            sums.append(product(high, table_high) + product(high, table_low) + product(low, table_high))
        by_re, by_im = sums
        results = []
        for j in range(len(pairs)):
            re_rows = slice(2 * j * window, (2 * j + 1) * window)
            im_rows = slice((2 * j + 1) * window, (2 * j + 2) * window)
            if sign > 0:
                results.append((by_re[re_rows] - by_im[im_rows], by_im[re_rows] + by_re[im_rows]))
            else:
                results.append((by_re[re_rows] + by_im[im_rows], by_re[im_rows] - by_im[re_rows]))
        return results

    def times(x, y):
        return x[0] * y[0] - x[1] * y[1], x[0] * y[1] + x[1] * y[0]

    def conj_times(x, y):
        return x[0] * y[0] + x[1] * y[1], x[0] * y[1] - x[1] * y[0]

    lane = lax.broadcasted_iota(jnp.int32, (window, 128), 1)

    def over_modes(value):
        total = value[:, :128]
        for start in range(128, width, 128):
            total = total + value[:, start : start + 128]
        return total + pltpu.roll(total, window, 1)

    def widened(value):
        return jnp.concatenate([value] * (width // 128), axis=1)

    def window_of(source, part, layer, j):
        rows = source[part, layer, pl.ds(rows_ref[j], window), :]
        rows = pltpu.roll(rows, lax.rem(size - cols_ref[j], size), 1)
        return widened(jnp.where(lane < window, rows, pltpu.roll(rows, window, 1)))

    def total_of(value):
        return jnp.sum(jnp.sum(value, axis=0, keepdims=True), axis=1, keepdims=True)

    spread[...] = jnp.zeros_like(spread)

    def placed(buffer, value, j):
        spread[buffer, pl.ds(size - window, window), :] = jnp.where(lane < window, value, 0.0)
        rows = spread[buffer, pl.ds(size - window - rows_ref[j], size), :]
        return pltpu.roll(rows, cols_ref[j], 1)

    def unfold_amps():
        first = lax.broadcasted_iota(jnp.int32, (slots, 128), 1) < window
        for i in range(window * window // 128):
            pair = amps_raw[:, pl.ds(128 * i, 128)]
            turned = pltpu.roll(pair, window, 1)
            amps_ref[:, 2 * i, :] = jnp.where(first, pair, turned)
            amps_ref[:, 2 * i + 1, :] = jnp.where(first, turned, pair)

    rim_rows = (pl.ds(0, BORDER), pl.ds(size - BORDER, BORDER))
    rim_plan = (
        (0, -1, 0, s > 0, s < n_strip - 1),
        (0, -1, -1, (s > 0) & (b > 0), (s < n_strip - 1) & (b < n_blk - 1)),
        (1, 1, 0, s < n_strip - 1, s > 0),
        (1, 1, 1, (s < n_strip - 1) & (b < n_blk - 1), (s > 0) & (b > 0)),
    )

    def rim_copy(layer, kind):
        edge, ds, db, _, _ = rim_plan[kind]
        return pltpu.make_async_remote_copy(
            src_ref=tile.at[:, layer, rim_rows[edge], :],
            dst_ref=rims.at[kind, layer],
            send_sem=rim_send.at[kind, layer],
            recv_sem=rim_recv.at[kind, layer],
            device_id=(strip_step(ds), blk_step(db)),
            device_id_type=MESH,
        )

    def send_rims(layer):
        for kind in range(4):
            @pl.when(rim_plan[kind][3])
            def _():
                rim_copy(layer, kind).start()

    ring = pltpu.make_async_remote_copy(
        src_ref=probe_out, dst_ref=probe_in,
        send_sem=ring_sems.at[0], recv_sem=ring_sems.at[1],
        device_id=(s, blk_step(1)), device_id_type=MESH,
    )

    for round_index in range(ROUNDS):
        last = round_index == ROUNDS - 1
        source = objects_ref if round_index == 0 else tile
        probe_src = probe_ref if round_index == 0 else probe_in
        if round_index == 0:
            loads[0].wait()
        powers = []
        for layer in range(2):
            squares = source[0, layer] ** 2 + source[1, layer] ** 2
            powers.append(total_of(squares) / (size * size) + power_epsilon)
        objects = [
            [(window_of(source, 0, layer, j), window_of(source, 1, layer, j)) for j in range(slots)]
            for layer in range(2)
        ]
        if round_index > 0:
            ring.wait_recv()
        else:
            for load in loads[1:4]:
                load.wait()
        probe = (probe_src[0], probe_src[1])
        probe_power = total_of(probe[0] ** 2 + probe[1] ** 2) / (window * window) + power_epsilon
        arrivals = transform([times(probe, objects[0][j]) for j in range(slots)], 4, 4, 1)
        if round_index == 0:
            for load in loads[4:]:
                load.wait()
            unfold_amps()
        far = transform([times(arrivals[j], objects[1][j]) for j in range(slots)], 0, 0, 1)
        changes = []
        for j in range(slots):
            weight = jnp.where(counts_ref[0] > j, 1.0, 0.0)
            modulus = jnp.sqrt(over_modes(far[j][0] ** 2 + far[j][1] ** 2))
            factor = widened((amps_ref[j] / jnp.maximum(modulus, modulus_floor) - 1.0) * weight)
            changes.append((far[j][0] * factor, far[j][1] * factor))
        exits = transform(changes, 2, 0, -1)

        second_gain = object_rate / (probe_power * powers[0] * slots)
        for part in range(2):
            total = source[part, 1]
            for j in range(slots):
                update = over_modes(conj_times(arrivals[j], exits[j])[part]) * second_gain
                total = total + placed(2 * j + part, update, j)
            tile[part, 1] = total
        if last:
            send_rims(1)

        entries = transform([conj_times(objects[1][j], exits[j]) for j in range(slots)], 6, 4, -1)
        probe_gain = probe_rate / (powers[0] * powers[1] * slots)
        terms = [conj_times(objects[0][j], entries[j]) for j in range(slots)]
        moved = []
        for part in range(2):
            total = terms[0][part]
            for j in range(1, slots):
                total = total + terms[j][part]
            moved.append(probe[part] + probe_gain * total)
        if not last:
            for part in range(2):
                probe_out[part] = moved[part]
            if round_index == 0:
                pl.semaphore_wait(barrier, len(partners))
            ring.start()
        else:
            stacked = jnp.concatenate([moved[0] - probe_ref[0], moved[1] - probe_ref[1]], axis=0)
            group_of = lax.broadcasted_iota(jnp.int32, (share, 128), 1) // share
            for h in range(width // 128):
                for i in range(groups):
                    packed = None
                    for k in range(groups):
                        block = stacked[k * share : (k + 1) * share, h * 128 : (h + 1) * 128]
                        if k != i:
                            block = pltpu.roll(block, (k - i) % groups * share, 1)
                        packed = block if packed is None else jnp.where(group_of == k, block, packed)
                    shares[h * groups + i] = packed
            share_copies = []
            for k in range(1, n_blk):
                share_copies.append(
                    pltpu.make_async_remote_copy(
                        src_ref=shares.at[blk_step(k)], dst_ref=arrived.at[k],
                        send_sem=share_send.at[k], recv_sem=share_recv.at[k],
                        device_id=(s, blk_step(k)), device_id_type=MESH,
                    )
                )
                share_copies[-1].start()

        first_gain = object_rate / (probe_power * slots)
        for part in range(2):
            total = source[part, 0]
            for j in range(slots):
                update = over_modes(conj_times(probe, entries[j])[part]) * first_gain
                total = total + placed(2 * j + part, update, j)
            tile[part, 0] = total
        if last:
            send_rims(0)
        else:
            ring.wait_send()

    own = shares[b]
    for k in range(1, n_blk):
        share_copies[k - 1].wait_recv()
        own = own + arrived[k]
    partial[...] = own
    strip_copies = []
    for k in range(1, n_strip):
        strip_copies.append(
            pltpu.make_async_remote_copy(
                src_ref=partial, dst_ref=strips.at[k],
                send_sem=strip_send.at[k], recv_sem=strip_recv.at[k],
                device_id=(strip_step(k), b), device_id_type=MESH,
            )
        )
        strip_copies[-1].start()

    for part in range(2):
        for layer in range(2):
            out_ref[part, layer, pl.ds(BORDER, size - 2 * BORDER), :] = tile[
                part, layer, pl.ds(BORDER, size - 2 * BORDER), :
            ]
    for layer in (1, 0):
        for kind in range(4):
            @pl.when(rim_plan[kind][4])
            def _():
                rim_copy(layer, kind).wait_recv()
    column = lax.broadcasted_iota(jnp.int32, (BORDER, size), 1)
    down = offsets_ref[s]
    up = offsets_ref[jnp.maximum(s - 1, 0)]
    for layer in range(2):
        for part in range(2):
            partner = pltpu.roll(
                jnp.where(column >= down, rims[0, layer, part], rims[1, layer, part]),
                lax.rem(size - down, size), 1,
            )
            valid = (s < n_strip - 1) & ((b < n_blk - 1) | (column + down < size))
            mine = tile[part, layer, rim_rows[1], :]
            out_ref[part, layer, rim_rows[1], :] = jnp.where(valid, 0.5 * (mine + partner), mine)
            partner = pltpu.roll(
                jnp.where(column < size - up, rims[2, layer, part], rims[3, layer, part]), up, 1
            )
            valid = (s > 0) & ((b > 0) | (column >= up))
            mine = tile[part, layer, rim_rows[0], :]
            out_ref[part, layer, rim_rows[0], :] = jnp.where(valid, 0.5 * (mine + partner), mine)

    total = partial[...]
    for k in range(1, n_strip):
        strip_copies[k - 1].wait_recv()
        total = total + strips[k]
    total = total / (n_strip * n_blk)
    for k in range(groups):
        block = total if k == 0 else pltpu.roll(total, (groups - k) * share, 1)
        part, row = divmod(k * share, window)
        step_ref[part, pl.ds(row, share), :] = block[:, :share]

    for copy in share_copies + strip_copies:
        copy.wait_send()
    for layer in range(2):
        for kind in range(4):
            @pl.when(rim_plan[kind][3])
            def _():
                rim_copy(layer, kind).wait_send()


def shards(n_strip, n_blk, objects, probe_init, scan_rows, scan_cols, amplitudes, counts, offsets):
    window, width = probe_init.shape[1], probe_init.shape[2]
    slots = scan_rows.shape[0]
    size = objects.shape[2]
    share = width // n_blk
    left, right = tables_of(window, width // window)
    smem = pl.BlockSpec(memory_space=pltpu.SMEM)
    vmem = pl.BlockSpec(memory_space=pltpu.VMEM)
    dma = pltpu.SemaphoreType.DMA
    return pl.pallas_call(
        functools.partial(kernel, n_strip, n_blk),
        out_shape=(
            pltpu.VMEM(objects.shape, jnp.float32),
            pltpu.VMEM((2, window, share), jnp.float32),
        ),
        in_specs=[smem] * 4 + [pl.BlockSpec(memory_space=pltpu.HBM)] * 5,
        out_specs=(vmem, vmem),
        scratch_shapes=[
            pltpu.VMEM(objects.shape, jnp.float32),
            pltpu.VMEM(probe_init.shape, jnp.float32),
            pltpu.VMEM(amplitudes.shape, jnp.float32),
            pltpu.VMEM(left.shape, jnp.bfloat16),
            pltpu.VMEM(right.shape, jnp.bfloat16),
            pltpu.VMEM((slots, window, 128), jnp.float32),
            dma((7,)),
            pltpu.VMEM(objects.shape, jnp.float32),
            pltpu.VMEM((2 * slots, 2 * size - window, size), jnp.float32),
            pltpu.VMEM(probe_init.shape, jnp.float32),
            pltpu.VMEM(probe_init.shape, jnp.float32),
            pltpu.VMEM((n_blk, share, 128), jnp.float32),
            pltpu.VMEM((n_blk, share, 128), jnp.float32),
            pltpu.VMEM((share, 128), jnp.float32),
            pltpu.VMEM((n_strip, share, 128), jnp.float32),
            pltpu.VMEM((4, 2, 2, BORDER, size), jnp.float32),
            dma((2,)),
            dma((n_blk,)), dma((n_blk,)),
            dma((n_strip,)), dma((n_strip,)),
            dma((4, 2)), dma((4, 2)),
        ],
        compiler_params=pltpu.CompilerParams(
            collective_id=0, has_side_effects=True, vmem_limit_bytes=60 * 1024 * 1024
        ),
    )(
        scan_rows, scan_cols, counts, offsets,
        objects, probe_init, amplitudes,
        jnp.asarray(left), jnp.asarray(right),
    )


def solution(mesh):
    return jax.shard_map(
        functools.partial(shards, mesh.shape["strip"], mesh.shape["blk"]),
        mesh=mesh,
        in_specs=(
            P(None, None, "strip", "blk"),
            P(),
            P(("strip", "blk")),
            P(("strip", "blk")),
            P(("strip", "blk"), None),
            P(("strip", "blk")),
            P(),
        ),
        out_specs=(P(None, None, "strip", "blk"), P(None, None, "blk")),
        check_vma=False,
    )
```

```python
import functools

import jax
import jax.numpy as jnp
import ml_dtypes
import numpy as np
from jax import lax
from jax.experimental import pallas as pl
from jax.experimental.pallas import tpu as pltpu
from jax.sharding import PartitionSpec as P

ROUNDS = 2
BORDER = 32
object_rate = 0.3
probe_rate = 0.5
modulus_floor = 0.25
fresnel_phase = 0.15
power_epsilon = 1e-06
MESH = pl.DeviceIdType.MESH


def two_parts(table):
    high = table.astype(ml_dtypes.bfloat16)
    low = (table - high.astype(np.float64)).astype(ml_dtypes.bfloat16)
    return high, low


def tables_of(window, modes):
    position = np.arange(window)
    angle = (position[:, None] * position[None, :] % window) * (2 * np.pi / window)
    dft = (np.cos(angle) - 1j * np.sin(angle)) / np.sqrt(window)
    frequency = np.where(position < window // 2, position, position - window)
    phase = np.exp(1j * fresnel_phase * frequency.astype(np.float64) ** 2 / window)
    fresnel = np.conj(dft) @ (phase[:, None] * dft)
    tables = []
    for matrix in (fresnel, dft, np.conj(dft), np.conj(fresnel)):
        high, low = two_parts(np.block([[matrix.real, -matrix.imag], [matrix.imag, matrix.real]]))
        pair = np.kron(np.eye(128 // window), matrix)
        tables.append(np.block([[high, high], [low, low]]))
        tables += two_parts(np.block([[pair.real, pair.imag], [-pair.imag, pair.real]]))
    return np.stack(tables).astype(ml_dtypes.bfloat16)


def halves(value):
    high = value.astype(jnp.bfloat16)
    return high, (value - high.astype(jnp.float32)).astype(jnp.bfloat16)


def product(left, right):
    return jnp.dot(left, right, preferred_element_type=jnp.float32)


def kernel(
    n_strip, n_blk,
    rows_ref, cols_ref, counts_ref, offsets_ref,
    objects_hbm, probe_hbm, amps_hbm, tables_hbm,
    out_ref, step_ref,
    objects_ref, probe_ref, amps_raw, tables, amps_ref, in_sems,
    tile, spread, probe_out, probe_in,
    shares, arrived, partial, strips, rims,
    ring_sems, share_send, share_recv, strip_send, strip_recv, rim_send, rim_recv,
):
    s, b = lax.axis_index("strip"), lax.axis_index("blk")
    window, width = probe_ref.shape[1], probe_ref.shape[2]
    modes = width // window
    slots = amps_ref.shape[0]
    size = objects_ref.shape[2]
    loads = [
        pltpu.make_async_copy(source, target, in_sems.at[i])
        for i, (source, target) in enumerate((
            (objects_hbm, objects_ref),
            (probe_hbm, probe_ref),
            (amps_hbm, amps_raw),
            *((tables_hbm.at[pl.ds(3 * i, 3)], tables.at[pl.ds(3 * i, 3)]) for i in range(4)),
        ))
    ]
    for load in loads:
        load.start()
    share = shares.shape[1]
    groups = 128 // share
    n_pairs = width // 128

    def blk_step(k):
        return lax.rem(b + k + n_blk, n_blk)

    def strip_step(k):
        return lax.rem(s + k + n_strip, n_strip)

    rims[...] = jnp.zeros_like(rims)
    barrier = pltpu.get_barrier_semaphore()
    partners = [(s, blk_step(k)) for k in range(1, n_blk)]
    partners += [(strip_step(k), b) for k in range(1, n_strip)]
    partners += [(strip_step(k), blk_step(k)) for k in (-1, 1)]
    for partner in partners:
        pl.semaphore_signal(barrier, inc=1, device_id=partner, device_id_type=MESH)

    def left_side(pairs, index):
        middles = []
        for re, im in pairs:
            stacked = jnp.concatenate(halves(jnp.concatenate([re, im], axis=0)), axis=0)
            both = product(tables[3 * index], stacked)
            total = both[: 2 * window] + both[2 * window :]
            middles.append((total[:window], total[window:]))
        return middles

    def right_side(pairs, index):
        rows = pairs[0][0].shape[0]
        blocks = []
        for re, im in pairs:
            for start in range(0, width, 128):
                blocks.append(jnp.concatenate([re[:, start : start + 128], im[:, start : start + 128]], axis=1))
        high, low = halves(jnp.concatenate(blocks, axis=0))
        count = high.shape[0]
        both = product(jnp.concatenate([high, low], axis=0), tables[3 * index + 1])
        total = both[:count] + both[count:] + product(high, tables[3 * index + 2])
        results = []
        for j in range(len(pairs)):
            mine = [total[(j * n_pairs + p) * rows : (j * n_pairs + p + 1) * rows] for p in range(n_pairs)]
            results.append(tuple(
                jnp.concatenate([x[:, part * 128 : (part + 1) * 128] for x in mine], axis=1) for part in range(2)
            ))
        return results

    def transform(pairs, index):
        return [right_side(left_side([pair], index), index)[0] for pair in pairs]

    def times(x, y):
        return x[0] * y[0] - x[1] * y[1], x[0] * y[1] + x[1] * y[0]

    def conj_times(x, y):
        return x[0] * y[0] + x[1] * y[1], x[0] * y[1] - x[1] * y[0]

    lane = lax.broadcasted_iota(jnp.int32, (window, 128), 1)

    def over_modes(value):
        total = value[:, :128]
        for start in range(128, width, 128):
            total = total + value[:, start : start + 128]
        return total + pltpu.roll(total, window, 1)

    def widened(value):
        return jnp.concatenate([value] * (width // 128), axis=1)

    def window_of(source, part, layer, j):
        rows = source[part, layer, pl.ds(rows_ref[j], window), :]
        rows = pltpu.roll(rows, lax.rem(size - cols_ref[j], size), 1)
        return widened(jnp.where(lane < window, rows, pltpu.roll(rows, window, 1)))

    def total_of(value):
        return jnp.sum(jnp.sum(value, axis=0, keepdims=True), axis=1, keepdims=True)

    spread[...] = jnp.zeros_like(spread)

    def placed(buffer, value, j):
        spread[buffer, pl.ds(size - window, window), :] = jnp.where(lane < window, value, 0.0)
        rows = spread[buffer, pl.ds(size - window - rows_ref[j], size), :]
        return pltpu.roll(rows, cols_ref[j], 1)

    def unfold_amps():
        first = lax.broadcasted_iota(jnp.int32, (slots, 128), 1) < window
        for i in range(window * window // 128):
            pair = amps_raw[:, pl.ds(128 * i, 128)]
            turned = pltpu.roll(pair, window, 1)
            amps_ref[:, 2 * i, :] = jnp.where(first, pair, turned)
            amps_ref[:, 2 * i + 1, :] = jnp.where(first, turned, pair)

    rim_rows = (pl.ds(0, BORDER), pl.ds(size - BORDER, BORDER))
    rim_plan = (
        (0, -1, 0, s > 0, s < n_strip - 1),
        (0, -1, -1, (s > 0) & (b > 0), (s < n_strip - 1) & (b < n_blk - 1)),
        (1, 1, 0, s < n_strip - 1, s > 0),
        (1, 1, 1, (s < n_strip - 1) & (b < n_blk - 1), (s > 0) & (b > 0)),
    )

    def rim_copy(layer, kind):
        edge, ds, db, _, _ = rim_plan[kind]
        return pltpu.make_async_remote_copy(
            src_ref=tile.at[:, layer, rim_rows[edge], :],
            dst_ref=rims.at[kind, layer],
            send_sem=rim_send.at[kind, layer],
            recv_sem=rim_recv.at[kind, layer],
            device_id=(strip_step(ds), blk_step(db)),
            device_id_type=MESH,
        )

    def send_rims(layer):
        for kind in range(4):
            @pl.when(rim_plan[kind][3])
            def _():
                rim_copy(layer, kind).start()

    ring = pltpu.make_async_remote_copy(
        src_ref=probe_out, dst_ref=probe_in,
        send_sem=ring_sems.at[0], recv_sem=ring_sems.at[1],
        device_id=(s, blk_step(1)), device_id_type=MESH,
    )

    for round_index in range(ROUNDS):
        last = round_index == ROUNDS - 1
        source = objects_ref if round_index == 0 else tile
        probe_src = probe_ref if round_index == 0 else probe_in
        if round_index == 0:
            loads[0].wait()
        powers = []
        for layer in range(2):
            squares = source[0, layer] ** 2 + source[1, layer] ** 2
            powers.append(total_of(squares) / (size * size) + power_epsilon)
        objects = [
            [(window_of(source, 0, layer, j), window_of(source, 1, layer, j)) for j in range(slots)]
            for layer in range(2)
        ]
        if round_index > 0:
            ring.wait_recv()
            ring.wait_send()
        else:
            loads[1].wait()
            loads[3].wait()
        probe = (probe_src[0], probe_src[1])
        probe_power = total_of(probe[0] ** 2 + probe[1] ** 2) / (window * window) + power_epsilon
        arrivals = transform([times(probe, objects[0][j]) for j in range(slots)], 0)
        if round_index == 0:
            loads[2].wait()
            unfold_amps()
            loads[4].wait()
        far = transform([times(arrivals[j], objects[1][j]) for j in range(slots)], 1)
        changes = []
        for j in range(slots):
            weight = jnp.where(counts_ref[0] > j, 1.0, 0.0)
            modulus = jnp.sqrt(over_modes(far[j][0] ** 2 + far[j][1] ** 2))
            factor = widened((amps_ref[j] / jnp.maximum(modulus, modulus_floor) - 1.0) * weight)
            changes.append((far[j][0] * factor, far[j][1] * factor))
        if round_index == 0:
            loads[5].wait()
        exits = transform(changes, 2)

        second_gain = object_rate / (probe_power * powers[0] * slots)
        for part in range(2):
            total = source[part, 1]
            for j in range(slots):
                update = over_modes(conj_times(arrivals[j], exits[j])[part]) * second_gain
                total = total + placed(2 * j + part, update, j)
            tile[part, 1] = total
        if last:
            send_rims(1)

        if round_index == 0:
            loads[6].wait()
        entries = transform([conj_times(objects[1][j], exits[j]) for j in range(slots)], 3)
        probe_gain = probe_rate / (powers[0] * powers[1] * slots)
        terms = [conj_times(objects[0][j], entries[j]) for j in range(slots)]
        moved = []
        for part in range(2):
            total = terms[0][part]
            for j in range(1, slots):
                total = total + terms[j][part]
            moved.append(probe[part] + probe_gain * total)
        if not last:
            for part in range(2):
                probe_out[part] = moved[part]
            if round_index == 0:
                pl.semaphore_wait(barrier, len(partners))
            ring.start()
        else:
            stacked = jnp.concatenate([moved[0] - probe_ref[0], moved[1] - probe_ref[1]], axis=0)
            group_of = lax.broadcasted_iota(jnp.int32, (share, 128), 1) // share
            for h in range(width // 128):
                for i in range(groups):
                    packed = None
                    for k in range(groups):
                        block = stacked[k * share : (k + 1) * share, h * 128 : (h + 1) * 128]
                        if k != i:
                            block = pltpu.roll(block, (k - i) % groups * share, 1)
                        packed = block if packed is None else jnp.where(group_of == k, block, packed)
                    shares[h * groups + i] = packed
            share_copies = []
            for k in range(1, n_blk):
                share_copies.append(
                    pltpu.make_async_remote_copy(
                        src_ref=shares.at[blk_step(k)], dst_ref=arrived.at[k],
                        send_sem=share_send.at[k], recv_sem=share_recv.at[k],
                        device_id=(s, blk_step(k)), device_id_type=MESH,
                    )
                )
                share_copies[-1].start()

        first_gain = object_rate / (probe_power * slots)
        for part in range(2):
            total = source[part, 0]
            for j in range(slots):
                update = over_modes(conj_times(probe, entries[j])[part]) * first_gain
                total = total + placed(2 * j + part, update, j)
            tile[part, 0] = total
        if last:
            send_rims(0)

    own = shares[b]
    for k in range(1, n_blk):
        share_copies[k - 1].wait_recv()
        own = own + arrived[k]
    partial[...] = own
    strip_copies = []
    for k in range(1, n_strip):
        strip_copies.append(
            pltpu.make_async_remote_copy(
                src_ref=partial, dst_ref=strips.at[k],
                send_sem=strip_send.at[k], recv_sem=strip_recv.at[k],
                device_id=(strip_step(k), b), device_id_type=MESH,
            )
        )
        strip_copies[-1].start()

    for part in range(2):
        for layer in range(2):
            out_ref[part, layer, pl.ds(BORDER, size - 2 * BORDER), :] = tile[
                part, layer, pl.ds(BORDER, size - 2 * BORDER), :
            ]
    for layer in (1, 0):
        for kind in range(4):
            @pl.when(rim_plan[kind][4])
            def _():
                rim_copy(layer, kind).wait_recv()
    column = lax.broadcasted_iota(jnp.int32, (BORDER, size), 1)
    down = offsets_ref[s]
    up = offsets_ref[jnp.maximum(s - 1, 0)]
    for layer in range(2):
        for part in range(2):
            partner = pltpu.roll(
                jnp.where(column >= down, rims[0, layer, part], rims[1, layer, part]),
                lax.rem(size - down, size), 1,
            )
            valid = (s < n_strip - 1) & ((b < n_blk - 1) | (column + down < size))
            mine = tile[part, layer, rim_rows[1], :]
            out_ref[part, layer, rim_rows[1], :] = jnp.where(valid, 0.5 * (mine + partner), mine)
            partner = pltpu.roll(
                jnp.where(column < size - up, rims[2, layer, part], rims[3, layer, part]), up, 1
            )
            valid = (s > 0) & ((b > 0) | (column >= up))
            mine = tile[part, layer, rim_rows[0], :]
            out_ref[part, layer, rim_rows[0], :] = jnp.where(valid, 0.5 * (mine + partner), mine)

    total = partial[...]
    for k in range(1, n_strip):
        strip_copies[k - 1].wait_recv()
        total = total + strips[k]
    total = total / (n_strip * n_blk)
    for k in range(groups):
        block = total if k == 0 else pltpu.roll(total, (groups - k) * share, 1)
        part, row = divmod(k * share, window)
        step_ref[part, pl.ds(row, share), :] = block[:, :share]

    for copy in share_copies + strip_copies:
        copy.wait_send()
    for layer in range(2):
        for kind in range(4):
            @pl.when(rim_plan[kind][3])
            def _():
                rim_copy(layer, kind).wait_send()


def shards(n_strip, n_blk, objects, probe_init, scan_rows, scan_cols, amplitudes, counts, offsets):
    window, width = probe_init.shape[1], probe_init.shape[2]
    slots = scan_rows.shape[0]
    size = objects.shape[2]
    share = width // n_blk
    tables = tables_of(window, width // window)
    smem = pl.BlockSpec(memory_space=pltpu.SMEM)
    vmem = pl.BlockSpec(memory_space=pltpu.VMEM)
    dma = pltpu.SemaphoreType.DMA
    return pl.pallas_call(
        functools.partial(kernel, n_strip, n_blk),
        out_shape=(
            pltpu.VMEM(objects.shape, jnp.float32),
            pltpu.VMEM((2, window, share), jnp.float32),
        ),
        in_specs=[smem] * 4 + [pl.BlockSpec(memory_space=pltpu.HBM)] * 4,
        out_specs=(vmem, vmem),
        scratch_shapes=[
            pltpu.VMEM(objects.shape, jnp.float32),
            pltpu.VMEM(probe_init.shape, jnp.float32),
            pltpu.VMEM(amplitudes.shape, jnp.float32),
            pltpu.VMEM(tables.shape, jnp.bfloat16),
            pltpu.VMEM((slots, window, 128), jnp.float32),
            dma((7,)),
            pltpu.VMEM(objects.shape, jnp.float32),
            pltpu.VMEM((2 * slots, 2 * size - window, size), jnp.float32),
            pltpu.VMEM(probe_init.shape, jnp.float32),
            pltpu.VMEM(probe_init.shape, jnp.float32),
            pltpu.VMEM((n_blk, share, 128), jnp.float32),
            pltpu.VMEM((n_blk, share, 128), jnp.float32),
            pltpu.VMEM((share, 128), jnp.float32),
            pltpu.VMEM((n_strip, share, 128), jnp.float32),
            pltpu.VMEM((4, 2, 2, BORDER, size), jnp.float32),
            dma((2,)),
            dma((n_blk,)), dma((n_blk,)),
            dma((n_strip,)), dma((n_strip,)),
            dma((4, 2)), dma((4, 2)),
        ],
        compiler_params=pltpu.CompilerParams(
            collective_id=0, has_side_effects=True, vmem_limit_bytes=60 * 1024 * 1024
        ),
    )(
        scan_rows, scan_cols, counts, offsets,
        objects, probe_init, amplitudes,
        jnp.asarray(tables),
    )


def solution(mesh):
    return jax.shard_map(
        functools.partial(shards, mesh.shape["strip"], mesh.shape["blk"]),
        mesh=mesh,
        in_specs=(
            P(None, None, "strip", "blk"),
            P(),
            P(("strip", "blk")),
            P(("strip", "blk")),
            P(("strip", "blk"), None),
            P(("strip", "blk")),
            P(),
        ),
        out_specs=(P(None, None, "strip", "blk"), P(None, None, "blk")),
        check_vma=False,
    )
```

```python
import functools

import jax
import jax.numpy as jnp
import ml_dtypes
import numpy as np
from jax import lax
from jax.experimental import pallas as pl
from jax.experimental.pallas import tpu as pltpu
from jax.sharding import PartitionSpec as P

ROUNDS = 2
BORDER = 32
RING_CHUNKS = 4
object_rate = 0.3
probe_rate = 0.5
modulus_floor = 0.25
fresnel_phase = 0.15
power_epsilon = 1e-06
MESH = pl.DeviceIdType.MESH


def two_parts(table):
    high = table.astype(ml_dtypes.bfloat16)
    low = (table - high.astype(np.float64)).astype(ml_dtypes.bfloat16)
    return high, low


def tables_of(window, modes):
    position = np.arange(window)
    angle = (position[:, None] * position[None, :] % window) * (2 * np.pi / window)
    dft = (np.cos(angle) - 1j * np.sin(angle)) / np.sqrt(window)
    frequency = np.where(position < window // 2, position, position - window)
    phase = np.exp(1j * fresnel_phase * frequency.astype(np.float64) ** 2 / window)
    fresnel = np.conj(dft) @ (phase[:, None] * dft)
    tables = []
    for matrix in (fresnel, dft, np.conj(dft), np.conj(fresnel)):
        high, low = two_parts(np.block([[matrix.real, -matrix.imag], [matrix.imag, matrix.real]]))
        pair = np.kron(np.eye(128 // window), matrix)
        tables.append(np.block([[high, high], [low, low]]))
        tables += two_parts(np.block([[pair.real, pair.imag], [-pair.imag, pair.real]]))
    return np.stack(tables).astype(ml_dtypes.bfloat16)


def halves(value):
    high = value.astype(jnp.bfloat16)
    return high, (value - high.astype(jnp.float32)).astype(jnp.bfloat16)


def product(left, right):
    return jnp.dot(left, right, preferred_element_type=jnp.float32)


def kernel(
    n_strip, n_blk,
    rows_ref, cols_ref, counts_ref, offsets_ref,
    objects_hbm, probe_hbm, amps_hbm, tables_hbm,
    out_ref, step_ref,
    objects_ref, probe_ref, amps_raw, tables, amps_ref, in_sems,
    tile, spread, probe_out, probe_in,
    shares, arrived, partial, strips, rims,
    ring_sems, share_send, share_recv, strip_send, strip_recv, rim_send, rim_recv,
):
    s, b = lax.axis_index("strip"), lax.axis_index("blk")
    window, width = probe_ref.shape[1], probe_ref.shape[2]
    modes = width // window
    slots = amps_ref.shape[0]
    size = objects_ref.shape[2]
    loads = [
        pltpu.make_async_copy(source, target, in_sems.at[i])
        for i, (source, target) in enumerate((
            (objects_hbm, objects_ref),
            (probe_hbm, probe_ref),
            (amps_hbm, amps_raw),
            *((tables_hbm.at[pl.ds(3 * i, 3)], tables.at[pl.ds(3 * i, 3)]) for i in range(4)),
        ))
    ]
    for load in loads:
        load.start()
    share = shares.shape[1]
    groups = 128 // share
    n_pairs = width // 128

    def blk_step(k):
        return lax.rem(b + k + n_blk, n_blk)

    def strip_step(k):
        return lax.rem(s + k + n_strip, n_strip)

    rims[...] = jnp.zeros_like(rims)
    barrier = pltpu.get_barrier_semaphore()
    partners = [(s, blk_step(k)) for k in range(1, n_blk)]
    partners += [(strip_step(k), b) for k in range(1, n_strip)]
    partners += [(strip_step(k), blk_step(k)) for k in (-1, 1)]
    for partner in partners:
        pl.semaphore_signal(barrier, inc=1, device_id=partner, device_id_type=MESH)

    def left_side(pairs, index):
        middles = []
        for re, im in pairs:
            stacked = jnp.concatenate(halves(jnp.concatenate([re, im], axis=0)), axis=0)
            both = product(tables[3 * index], stacked)
            total = both[: 2 * window] + both[2 * window :]
            middles.append((total[:window], total[window:]))
        return middles

    def right_side(pairs, index):
        rows = pairs[0][0].shape[0]
        blocks = []
        for re, im in pairs:
            for start in range(0, width, 128):
                blocks.append(jnp.concatenate([re[:, start : start + 128], im[:, start : start + 128]], axis=1))
        high, low = halves(jnp.concatenate(blocks, axis=0))
        count = high.shape[0]
        both = product(jnp.concatenate([high, low], axis=0), tables[3 * index + 1])
        total = both[:count] + both[count:] + product(high, tables[3 * index + 2])
        results = []
        for j in range(len(pairs)):
            mine = [total[(j * n_pairs + p) * rows : (j * n_pairs + p + 1) * rows] for p in range(n_pairs)]
            results.append(tuple(
                jnp.concatenate([x[:, part * 128 : (part + 1) * 128] for x in mine], axis=1) for part in range(2)
            ))
        return results

    def transform(pairs, index):
        return [right_side(left_side([pair], index), index)[0] for pair in pairs]

    def times(x, y):
        return x[0] * y[0] - x[1] * y[1], x[0] * y[1] + x[1] * y[0]

    def conj_times(x, y):
        return x[0] * y[0] + x[1] * y[1], x[0] * y[1] - x[1] * y[0]

    lane = lax.broadcasted_iota(jnp.int32, (window, 128), 1)

    def over_modes(value):
        total = value[:, :128]
        for start in range(128, width, 128):
            total = total + value[:, start : start + 128]
        return total + pltpu.roll(total, window, 1)

    def widened(value):
        return jnp.concatenate([value] * (width // 128), axis=1)

    def window_of(source, part, layer, j):
        rows = source[part, layer, pl.ds(rows_ref[j], window), :]
        rows = pltpu.roll(rows, lax.rem(size - cols_ref[j], size), 1)
        return widened(jnp.where(lane < window, rows, pltpu.roll(rows, window, 1)))

    def total_of(value):
        return jnp.sum(jnp.sum(value, axis=0, keepdims=True), axis=1, keepdims=True)

    spread[...] = jnp.zeros_like(spread)

    def placed(buffer, value, j):
        spread[buffer, pl.ds(size - window, window), :] = jnp.where(lane < window, value, 0.0)
        rows = spread[buffer, pl.ds(size - window - rows_ref[j], size), :]
        return pltpu.roll(rows, cols_ref[j], 1)

    def unfold_amps():
        first = lax.broadcasted_iota(jnp.int32, (slots, 128), 1) < window
        for i in range(window * window // 128):
            pair = amps_raw[:, pl.ds(128 * i, 128)]
            turned = pltpu.roll(pair, window, 1)
            amps_ref[:, 2 * i, :] = jnp.where(first, pair, turned)
            amps_ref[:, 2 * i + 1, :] = jnp.where(first, turned, pair)

    rim_rows = (pl.ds(0, BORDER), pl.ds(size - BORDER, BORDER))
    rim_plan = (
        (0, -1, 0, s > 0, s < n_strip - 1),
        (0, -1, -1, (s > 0) & (b > 0), (s < n_strip - 1) & (b < n_blk - 1)),
        (1, 1, 0, s < n_strip - 1, s > 0),
        (1, 1, 1, (s < n_strip - 1) & (b < n_blk - 1), (s > 0) & (b > 0)),
    )

    def rim_copy(layer, kind):
        edge, ds, db, _, _ = rim_plan[kind]
        return pltpu.make_async_remote_copy(
            src_ref=tile.at[:, layer, rim_rows[edge], :],
            dst_ref=rims.at[kind, layer],
            send_sem=rim_send.at[kind, layer],
            recv_sem=rim_recv.at[kind, layer],
            device_id=(strip_step(ds), blk_step(db)),
            device_id_type=MESH,
        )

    def send_rims(layer):
        for kind in range(4):
            @pl.when(rim_plan[kind][3])
            def _():
                rim_copy(layer, kind).start()

    chunk = window // RING_CHUNKS
    chunks = [slice(i * chunk, (i + 1) * chunk) for i in range(RING_CHUNKS)]

    def ring_copy(i):
        rows = pl.ds(i * chunk, chunk)
        return pltpu.make_async_remote_copy(
            src_ref=probe_out.at[:, rows, :], dst_ref=probe_in.at[:, rows, :],
            send_sem=ring_sems.at[0, i], recv_sem=ring_sems.at[1, i],
            device_id=(s, blk_step(1)), device_id_type=MESH,
        )

    ring = [ring_copy(i) for i in range(RING_CHUNKS)]

    def cut(pair, rows):
        return pair[0][rows], pair[1][rows]

    def joined(pieces):
        return tuple(jnp.concatenate([piece[part] for piece in pieces], axis=0) for part in range(2))

    for round_index in range(ROUNDS):
        last = round_index == ROUNDS - 1
        source = objects_ref if round_index == 0 else tile
        probe_src = probe_ref if round_index == 0 else probe_in
        if round_index == 0:
            loads[0].wait()
        powers = []
        for layer in range(2):
            squares = source[0, layer] ** 2 + source[1, layer] ** 2
            powers.append(total_of(squares) / (size * size) + power_epsilon)
        objects = [
            [(window_of(source, 0, layer, j), window_of(source, 1, layer, j)) for j in range(slots)]
            for layer in range(2)
        ]
        if round_index > 0:
            middles = []
            for i in range(RING_CHUNKS):
                ring[i].wait_recv()
                piece = (probe_in[0, pl.ds(i * chunk, chunk)], probe_in[1, pl.ds(i * chunk, chunk)])
                middles.append(right_side([times(piece, cut(objects[0][j], chunks[i])) for j in range(slots)], 0))
            arrivals = left_side([joined([piece[j] for piece in middles]) for j in range(slots)], 0)
            for copy in ring:
                copy.wait_send()
        else:
            loads[1].wait()
            loads[3].wait()
        probe = (probe_src[0], probe_src[1])
        probe_power = total_of(probe[0] ** 2 + probe[1] ** 2) / (window * window) + power_epsilon
        if round_index == 0:
            arrivals = transform([times(probe, objects[0][j]) for j in range(slots)], 0)
        if round_index == 0:
            loads[2].wait()
            unfold_amps()
            loads[4].wait()
        far = transform([times(arrivals[j], objects[1][j]) for j in range(slots)], 1)
        changes = []
        for j in range(slots):
            weight = jnp.where(counts_ref[0] > j, 1.0, 0.0)
            modulus = jnp.sqrt(over_modes(far[j][0] ** 2 + far[j][1] ** 2))
            factor = widened((amps_ref[j] / jnp.maximum(modulus, modulus_floor) - 1.0) * weight)
            changes.append((far[j][0] * factor, far[j][1] * factor))
        if round_index == 0:
            loads[5].wait()
        exits = transform(changes, 2)

        second_gain = object_rate / (probe_power * powers[0] * slots)
        for part in range(2):
            total = source[part, 1]
            for j in range(slots):
                update = over_modes(conj_times(arrivals[j], exits[j])[part]) * second_gain
                total = total + placed(2 * j + part, update, j)
            tile[part, 1] = total

        if round_index == 0:
            loads[6].wait()
        returns = [conj_times(objects[1][j], exits[j]) for j in range(slots)]
        probe_gain = probe_rate / (powers[0] * powers[1] * slots)

        def moved_probe(pieces, rows):
            terms = [conj_times(cut(objects[0][j], rows), pieces[j]) for j in range(slots)]
            moved = []
            for part in range(2):
                total = terms[0][part]
                for j in range(1, slots):
                    total = total + terms[j][part]
                moved.append(probe[part][rows] + probe_gain * total)
            return moved

        if not last:
            if round_index == 0:
                pl.semaphore_wait(barrier, len(partners))
            middles = left_side(returns, 3)
            pieces = []
            for i in range(RING_CHUNKS):
                pieces.append(right_side([cut(middle, chunks[i]) for middle in middles], 3))
                for part, value in enumerate(moved_probe(pieces[i], chunks[i])):
                    probe_out[part, pl.ds(i * chunk, chunk)] = value
                ring[i].start()
            entries = [joined([piece[j] for piece in pieces]) for j in range(slots)]
        else:
            entries = transform(returns, 3)
            moved = moved_probe(entries, slice(0, window))
            stacked = jnp.concatenate([moved[0] - probe_ref[0], moved[1] - probe_ref[1]], axis=0)
            group_of = lax.broadcasted_iota(jnp.int32, (share, 128), 1) // share
            for h in range(width // 128):
                for i in range(groups):
                    packed = None
                    for k in range(groups):
                        block = stacked[k * share : (k + 1) * share, h * 128 : (h + 1) * 128]
                        if k != i:
                            block = pltpu.roll(block, (k - i) % groups * share, 1)
                        packed = block if packed is None else jnp.where(group_of == k, block, packed)
                    shares[h * groups + i] = packed
            share_copies = []
            for k in range(1, n_blk):
                share_copies.append(
                    pltpu.make_async_remote_copy(
                        src_ref=shares.at[blk_step(k)], dst_ref=arrived.at[k],
                        send_sem=share_send.at[k], recv_sem=share_recv.at[k],
                        device_id=(s, blk_step(k)), device_id_type=MESH,
                    )
                )
                share_copies[-1].start()

        if last:
            send_rims(1)
        first_gain = object_rate / (probe_power * slots)
        for part in range(2):
            total = source[part, 0]
            for j in range(slots):
                update = over_modes(conj_times(probe, entries[j])[part]) * first_gain
                total = total + placed(2 * j + part, update, j)
            tile[part, 0] = total
        if last:
            send_rims(0)

    own = shares[b]
    for k in range(1, n_blk):
        share_copies[k - 1].wait_recv()
        own = own + arrived[k]
    partial[...] = own
    strip_copies = []
    for k in range(1, n_strip):
        strip_copies.append(
            pltpu.make_async_remote_copy(
                src_ref=partial, dst_ref=strips.at[k],
                send_sem=strip_send.at[k], recv_sem=strip_recv.at[k],
                device_id=(strip_step(k), b), device_id_type=MESH,
            )
        )
        strip_copies[-1].start()

    for part in range(2):
        for layer in range(2):
            out_ref[part, layer, pl.ds(BORDER, size - 2 * BORDER), :] = tile[
                part, layer, pl.ds(BORDER, size - 2 * BORDER), :
            ]
    for layer in (1, 0):
        for kind in range(4):
            @pl.when(rim_plan[kind][4])
            def _():
                rim_copy(layer, kind).wait_recv()
    column = lax.broadcasted_iota(jnp.int32, (BORDER, size), 1)
    down = offsets_ref[s]
    up = offsets_ref[jnp.maximum(s - 1, 0)]
    for layer in range(2):
        for part in range(2):
            partner = pltpu.roll(
                jnp.where(column >= down, rims[0, layer, part], rims[1, layer, part]),
                lax.rem(size - down, size), 1,
            )
            valid = (s < n_strip - 1) & ((b < n_blk - 1) | (column + down < size))
            mine = tile[part, layer, rim_rows[1], :]
            out_ref[part, layer, rim_rows[1], :] = jnp.where(valid, 0.5 * (mine + partner), mine)
            partner = pltpu.roll(
                jnp.where(column < size - up, rims[2, layer, part], rims[3, layer, part]), up, 1
            )
            valid = (s > 0) & ((b > 0) | (column >= up))
            mine = tile[part, layer, rim_rows[0], :]
            out_ref[part, layer, rim_rows[0], :] = jnp.where(valid, 0.5 * (mine + partner), mine)

    total = partial[...]
    for k in range(1, n_strip):
        strip_copies[k - 1].wait_recv()
        total = total + strips[k]
    total = total / (n_strip * n_blk)
    for k in range(groups):
        block = total if k == 0 else pltpu.roll(total, (groups - k) * share, 1)
        part, row = divmod(k * share, window)
        step_ref[part, pl.ds(row, share), :] = block[:, :share]

    for copy in share_copies + strip_copies:
        copy.wait_send()
    for layer in range(2):
        for kind in range(4):
            @pl.when(rim_plan[kind][3])
            def _():
                rim_copy(layer, kind).wait_send()


def shards(n_strip, n_blk, objects, probe_init, scan_rows, scan_cols, amplitudes, counts, offsets):
    window, width = probe_init.shape[1], probe_init.shape[2]
    slots = scan_rows.shape[0]
    size = objects.shape[2]
    share = width // n_blk
    tables = tables_of(window, width // window)
    smem = pl.BlockSpec(memory_space=pltpu.SMEM)
    vmem = pl.BlockSpec(memory_space=pltpu.VMEM)
    dma = pltpu.SemaphoreType.DMA
    return pl.pallas_call(
        functools.partial(kernel, n_strip, n_blk),
        out_shape=(
            pltpu.VMEM(objects.shape, jnp.float32),
            pltpu.VMEM((2, window, share), jnp.float32),
        ),
        in_specs=[smem] * 4 + [pl.BlockSpec(memory_space=pltpu.HBM)] * 4,
        out_specs=(vmem, vmem),
        scratch_shapes=[
            pltpu.VMEM(objects.shape, jnp.float32),
            pltpu.VMEM(probe_init.shape, jnp.float32),
            pltpu.VMEM(amplitudes.shape, jnp.float32),
            pltpu.VMEM(tables.shape, jnp.bfloat16),
            pltpu.VMEM((slots, window, 128), jnp.float32),
            dma((7,)),
            pltpu.VMEM(objects.shape, jnp.float32),
            pltpu.VMEM((2 * slots, 2 * size - window, size), jnp.float32),
            pltpu.VMEM(probe_init.shape, jnp.float32),
            pltpu.VMEM(probe_init.shape, jnp.float32),
            pltpu.VMEM((n_blk, share, 128), jnp.float32),
            pltpu.VMEM((n_blk, share, 128), jnp.float32),
            pltpu.VMEM((share, 128), jnp.float32),
            pltpu.VMEM((n_strip, share, 128), jnp.float32),
            pltpu.VMEM((4, 2, 2, BORDER, size), jnp.float32),
            dma((2, RING_CHUNKS)),
            dma((n_blk,)), dma((n_blk,)),
            dma((n_strip,)), dma((n_strip,)),
            dma((4, 2)), dma((4, 2)),
        ],
        compiler_params=pltpu.CompilerParams(
            collective_id=0, has_side_effects=True, vmem_limit_bytes=60 * 1024 * 1024
        ),
    )(
        scan_rows, scan_cols, counts, offsets,
        objects, probe_init, amplitudes,
        jnp.asarray(tables),
    )


def solution(mesh):
    return jax.shard_map(
        functools.partial(shards, mesh.shape["strip"], mesh.shape["blk"]),
        mesh=mesh,
        in_specs=(
            P(None, None, "strip", "blk"),
            P(),
            P(("strip", "blk")),
            P(("strip", "blk")),
            P(("strip", "blk"), None),
            P(("strip", "blk")),
            P(),
        ),
        out_specs=(P(None, None, "strip", "blk"), P(None, None, "blk")),
        check_vma=False,
    )
```

```python
import functools

import jax
import jax.numpy as jnp
import ml_dtypes
import numpy as np
from jax import lax
from jax.experimental import pallas as pl
from jax.experimental.pallas import tpu as pltpu
from jax.sharding import PartitionSpec as P

ROUNDS = 2
BORDER = 32
RING_CHUNKS = 4
object_rate = 0.3
probe_rate = 0.5
modulus_floor = 0.25
fresnel_phase = 0.15
power_epsilon = 1e-06
MESH = pl.DeviceIdType.MESH


def two_parts(table):
    high = table.astype(ml_dtypes.bfloat16)
    low = (table - high.astype(np.float64)).astype(ml_dtypes.bfloat16)
    return high, low


def tables_of(window, modes):
    position = np.arange(window)
    angle = (position[:, None] * position[None, :] % window) * (2 * np.pi / window)
    dft = (np.cos(angle) - 1j * np.sin(angle)) / np.sqrt(window)
    frequency = np.where(position < window // 2, position, position - window)
    phase = np.exp(1j * fresnel_phase * frequency.astype(np.float64) ** 2 / window)
    fresnel = np.conj(dft) @ (phase[:, None] * dft)
    tables = []
    for matrix in (fresnel, dft, np.conj(dft), np.conj(fresnel)):
        high, low = two_parts(np.block([[matrix.real, -matrix.imag], [matrix.imag, matrix.real]]))
        pair = np.kron(np.eye(128 // window), matrix)
        tables.append(np.block([[high, high], [low, low]]))
        tables += two_parts(np.block([[pair.real, pair.imag], [-pair.imag, pair.real]]))
    return np.stack(tables).astype(ml_dtypes.bfloat16)


def halves(value):
    high = value.astype(jnp.bfloat16)
    return high, (value - high.astype(jnp.float32)).astype(jnp.bfloat16)


def product(left, right):
    return jnp.dot(left, right, preferred_element_type=jnp.float32)


def kernel(
    n_strip, n_blk,
    rows_ref, cols_ref, counts_ref, offsets_ref,
    objects_hbm, probe_hbm, amps_hbm, tables_hbm,
    out_ref, step_ref,
    objects_ref, probe_ref, amps_raw, tables, amps_ref, in_sems,
    tile, spread, probe_out, probe_in,
    shares, arrived, partial, strips, rims,
    ring_sems, share_send, share_recv, strip_send, strip_recv, rim_send, rim_recv,
):
    s, b = lax.axis_index("strip"), lax.axis_index("blk")
    window, width = probe_ref.shape[1], probe_ref.shape[2]
    modes = width // window
    slots = amps_ref.shape[0]
    size = objects_ref.shape[2]
    loads = [
        pltpu.make_async_copy(source, target, in_sems.at[i])
        for i, (source, target) in enumerate((
            (objects_hbm, objects_ref),
            (probe_hbm, probe_ref),
            (amps_hbm, amps_raw),
            *((tables_hbm.at[pl.ds(3 * i, 3)], tables.at[pl.ds(3 * i, 3)]) for i in range(4)),
        ))
    ]
    for load in loads:
        load.start()
    share = shares.shape[1]
    groups = 128 // share
    n_pairs = width // 128

    def blk_step(k):
        return lax.rem(b + k + n_blk, n_blk)

    def strip_step(k):
        return lax.rem(s + k + n_strip, n_strip)

    rims[...] = jnp.zeros_like(rims)
    barrier = pltpu.get_barrier_semaphore()
    partners = [(s, blk_step(k)) for k in range(1, n_blk)]
    partners += [(strip_step(k), b) for k in range(1, n_strip)]
    partners += [(strip_step(k), blk_step(k)) for k in (-1, 1)]
    for partner in partners:
        pl.semaphore_signal(barrier, inc=1, device_id=partner, device_id_type=MESH)

    def left_side(pairs, index):
        middles = []
        for re, im in pairs:
            stacked = jnp.concatenate(halves(jnp.concatenate([re, im], axis=0)), axis=0)
            both = product(tables[3 * index], stacked)
            total = both[: 2 * window] + both[2 * window :]
            middles.append((total[:window], total[window:]))
        return middles

    def right_side(pairs, index):
        rows = pairs[0][0].shape[0]
        blocks = []
        for re, im in pairs:
            for start in range(0, width, 128):
                blocks.append(jnp.concatenate([re[:, start : start + 128], im[:, start : start + 128]], axis=1))
        high, low = halves(jnp.concatenate(blocks, axis=0))
        count = high.shape[0]
        both = product(jnp.concatenate([high, low], axis=0), tables[3 * index + 1])
        total = both[:count] + both[count:] + product(high, tables[3 * index + 2])
        results = []
        for j in range(len(pairs)):
            mine = [total[(j * n_pairs + p) * rows : (j * n_pairs + p + 1) * rows] for p in range(n_pairs)]
            results.append(tuple(
                jnp.concatenate([x[:, part * 128 : (part + 1) * 128] for x in mine], axis=1) for part in range(2)
            ))
        return results

    def transform(pairs, index):
        return [right_side(left_side([pair], index), index)[0] for pair in pairs]

    def times(x, y):
        return x[0] * y[0] - x[1] * y[1], x[0] * y[1] + x[1] * y[0]

    def conj_times(x, y):
        return x[0] * y[0] + x[1] * y[1], x[0] * y[1] - x[1] * y[0]

    lane = lax.broadcasted_iota(jnp.int32, (window, 128), 1)

    def over_modes(value):
        total = value[:, :128]
        for start in range(128, width, 128):
            total = total + value[:, start : start + 128]
        return total + pltpu.roll(total, window, 1)

    def widened(value):
        return jnp.concatenate([value] * (width // 128), axis=1)

    def window_of(source, part, layer, j):
        rows = source[part, layer, pl.ds(rows_ref[j], window), :]
        rows = pltpu.roll(rows, lax.rem(size - cols_ref[j], size), 1)
        return widened(jnp.where(lane < window, rows, pltpu.roll(rows, window, 1)))

    def total_of(value):
        return jnp.sum(jnp.sum(value, axis=0, keepdims=True), axis=1, keepdims=True)

    spread[...] = jnp.zeros_like(spread)

    def placed(buffer, value, j):
        spread[buffer, pl.ds(size - window, window), :] = jnp.where(lane < window, value, 0.0)
        rows = spread[buffer, pl.ds(size - window - rows_ref[j], size), :]
        return pltpu.roll(rows, cols_ref[j], 1)

    def unfold_amps():
        first = lax.broadcasted_iota(jnp.int32, (slots, 128), 1) < window
        for i in range(window * window // 128):
            pair = amps_raw[:, pl.ds(128 * i, 128)]
            turned = pltpu.roll(pair, window, 1)
            amps_ref[:, 2 * i, :] = jnp.where(first, pair, turned)
            amps_ref[:, 2 * i + 1, :] = jnp.where(first, turned, pair)

    rim_rows = (pl.ds(0, BORDER), pl.ds(size - BORDER, BORDER))
    rim_plan = (
        (0, -1, 0, s > 0, s < n_strip - 1),
        (0, -1, -1, (s > 0) & (b > 0), (s < n_strip - 1) & (b < n_blk - 1)),
        (1, 1, 0, s < n_strip - 1, s > 0),
        (1, 1, 1, (s < n_strip - 1) & (b < n_blk - 1), (s > 0) & (b > 0)),
    )

    def rim_copy(layer, kind):
        edge, ds, db, _, _ = rim_plan[kind]
        return pltpu.make_async_remote_copy(
            src_ref=tile.at[:, layer, rim_rows[edge], :],
            dst_ref=rims.at[kind, layer],
            send_sem=rim_send.at[kind, layer],
            recv_sem=rim_recv.at[kind, layer],
            device_id=(strip_step(ds), blk_step(db)),
            device_id_type=MESH,
        )

    def send_rims(layer):
        for kind in range(4):
            @pl.when(rim_plan[kind][3])
            def _():
                rim_copy(layer, kind).start()

    chunk = window // RING_CHUNKS
    chunks = [slice(i * chunk, (i + 1) * chunk) for i in range(RING_CHUNKS)]

    def ring_copy(i):
        rows = pl.ds(i * chunk, chunk)
        return pltpu.make_async_remote_copy(
            src_ref=probe_out.at[:, rows, :], dst_ref=probe_in.at[:, rows, :],
            send_sem=ring_sems.at[0, i], recv_sem=ring_sems.at[1, i],
            device_id=(s, blk_step(1)), device_id_type=MESH,
        )

    ring = [ring_copy(i) for i in range(RING_CHUNKS)]

    def cut(pair, rows):
        return pair[0][rows], pair[1][rows]

    def joined(pieces):
        return tuple(jnp.concatenate([piece[part] for piece in pieces], axis=0) for part in range(2))

    for round_index in range(ROUNDS):
        last = round_index == ROUNDS - 1
        source = objects_ref if round_index == 0 else tile
        probe_src = probe_ref if round_index == 0 else probe_in
        if round_index == 0:
            loads[0].wait()
        powers = []
        for layer in range(2):
            squares = source[0, layer] ** 2 + source[1, layer] ** 2
            powers.append(total_of(squares) / (size * size) + power_epsilon)
        objects = [
            [(window_of(source, 0, layer, j), window_of(source, 1, layer, j)) for j in range(slots)]
            for layer in range(2)
        ]
        if round_index > 0:
            middles = []
            for i in range(RING_CHUNKS):
                ring[i].wait_recv()
                piece = (probe_in[0, pl.ds(i * chunk, chunk)], probe_in[1, pl.ds(i * chunk, chunk)])
                middles.append(right_side([times(piece, cut(objects[0][j], chunks[i])) for j in range(slots)], 0))
            arrivals = left_side([joined([piece[j] for piece in middles]) for j in range(slots)], 0)
            for copy in ring:
                copy.wait_send()
        else:
            loads[1].wait()
            loads[3].wait()
        probe = (probe_src[0], probe_src[1])
        probe_power = total_of(probe[0] ** 2 + probe[1] ** 2) / (window * window) + power_epsilon
        if round_index == 0:
            arrivals = transform([times(probe, objects[0][j]) for j in range(slots)], 0)
        if round_index == 0:
            loads[2].wait()
            unfold_amps()
            loads[4].wait()
        far = transform([times(arrivals[j], objects[1][j]) for j in range(slots)], 1)
        changes = []
        for j in range(slots):
            weight = jnp.where(counts_ref[0] > j, 1.0, 0.0)
            modulus = jnp.sqrt(over_modes(far[j][0] ** 2 + far[j][1] ** 2))
            factor = widened((amps_ref[j] / jnp.maximum(modulus, modulus_floor) - 1.0) * weight)
            changes.append((far[j][0] * factor, far[j][1] * factor))
        if round_index == 0:
            loads[5].wait()
        exits = transform(changes, 2)

        if round_index == 0:
            loads[6].wait()
        returns = [conj_times(objects[1][j], exits[j]) for j in range(slots)]
        probe_gain = probe_rate / (powers[0] * powers[1] * slots)

        def moved_probe(pieces, rows):
            terms = [conj_times(cut(objects[0][j], rows), pieces[j]) for j in range(slots)]
            moved = []
            for part in range(2):
                total = terms[0][part]
                for j in range(1, slots):
                    total = total + terms[j][part]
                moved.append(probe[part][rows] + probe_gain * total)
            return moved

        if not last:
            if round_index == 0:
                pl.semaphore_wait(barrier, len(partners))
            middles = left_side(returns, 3)
            pieces = []
            for i in range(RING_CHUNKS):
                pieces.append(right_side([cut(middle, chunks[i]) for middle in middles], 3))
                for part, value in enumerate(moved_probe(pieces[i], chunks[i])):
                    probe_out[part, pl.ds(i * chunk, chunk)] = value
                ring[i].start()
            entries = [joined([piece[j] for piece in pieces]) for j in range(slots)]
        else:
            entries = transform(returns, 3)
            moved = moved_probe(entries, slice(0, window))
            stacked = jnp.concatenate([moved[0] - probe_ref[0], moved[1] - probe_ref[1]], axis=0)
            group_of = lax.broadcasted_iota(jnp.int32, (share, 128), 1) // share
            for h in range(width // 128):
                for i in range(groups):
                    packed = None
                    for k in range(groups):
                        block = stacked[k * share : (k + 1) * share, h * 128 : (h + 1) * 128]
                        if k != i:
                            block = pltpu.roll(block, (k - i) % groups * share, 1)
                        packed = block if packed is None else jnp.where(group_of == k, block, packed)
                    shares[h * groups + i] = packed
            share_copies = []
            for k in range(1, n_blk):
                share_copies.append(
                    pltpu.make_async_remote_copy(
                        src_ref=shares.at[blk_step(k)], dst_ref=arrived.at[k],
                        send_sem=share_send.at[k], recv_sem=share_recv.at[k],
                        device_id=(s, blk_step(k)), device_id_type=MESH,
                    )
                )
                share_copies[-1].start()

        second_gain = object_rate / (probe_power * powers[0] * slots)
        for part in range(2):
            total = source[part, 1]
            for j in range(slots):
                update = over_modes(conj_times(arrivals[j], exits[j])[part]) * second_gain
                total = total + placed(2 * j + part, update, j)
            tile[part, 1] = total
        if last:
            send_rims(1)
        first_gain = object_rate / (probe_power * slots)
        for part in range(2):
            total = source[part, 0]
            for j in range(slots):
                update = over_modes(conj_times(probe, entries[j])[part]) * first_gain
                total = total + placed(2 * j + part, update, j)
            tile[part, 0] = total
        if last:
            send_rims(0)

    own = shares[b]
    for k in range(1, n_blk):
        share_copies[k - 1].wait_recv()
        own = own + arrived[k]
    partial[...] = own
    strip_copies = []
    for k in range(1, n_strip):
        strip_copies.append(
            pltpu.make_async_remote_copy(
                src_ref=partial, dst_ref=strips.at[k],
                send_sem=strip_send.at[k], recv_sem=strip_recv.at[k],
                device_id=(strip_step(k), b), device_id_type=MESH,
            )
        )
        strip_copies[-1].start()

    for part in range(2):
        for layer in range(2):
            out_ref[part, layer, pl.ds(BORDER, size - 2 * BORDER), :] = tile[
                part, layer, pl.ds(BORDER, size - 2 * BORDER), :
            ]
    for layer in (1, 0):
        for kind in range(4):
            @pl.when(rim_plan[kind][4])
            def _():
                rim_copy(layer, kind).wait_recv()
    column = lax.broadcasted_iota(jnp.int32, (BORDER, size), 1)
    down = offsets_ref[s]
    up = offsets_ref[jnp.maximum(s - 1, 0)]
    for layer in range(2):
        for part in range(2):
            partner = pltpu.roll(
                jnp.where(column >= down, rims[0, layer, part], rims[1, layer, part]),
                lax.rem(size - down, size), 1,
            )
            valid = (s < n_strip - 1) & ((b < n_blk - 1) | (column + down < size))
            mine = tile[part, layer, rim_rows[1], :]
            out_ref[part, layer, rim_rows[1], :] = jnp.where(valid, 0.5 * (mine + partner), mine)
            partner = pltpu.roll(
                jnp.where(column < size - up, rims[2, layer, part], rims[3, layer, part]), up, 1
            )
            valid = (s > 0) & ((b > 0) | (column >= up))
            mine = tile[part, layer, rim_rows[0], :]
            out_ref[part, layer, rim_rows[0], :] = jnp.where(valid, 0.5 * (mine + partner), mine)

    total = partial[...]
    for k in range(1, n_strip):
        strip_copies[k - 1].wait_recv()
        total = total + strips[k]
    total = total / (n_strip * n_blk)
    for k in range(groups):
        block = total if k == 0 else pltpu.roll(total, (groups - k) * share, 1)
        part, row = divmod(k * share, window)
        step_ref[part, pl.ds(row, share), :] = block[:, :share]

    for copy in share_copies + strip_copies:
        copy.wait_send()
    for layer in range(2):
        for kind in range(4):
            @pl.when(rim_plan[kind][3])
            def _():
                rim_copy(layer, kind).wait_send()


def shards(n_strip, n_blk, objects, probe_init, scan_rows, scan_cols, amplitudes, counts, offsets):
    window, width = probe_init.shape[1], probe_init.shape[2]
    slots = scan_rows.shape[0]
    size = objects.shape[2]
    share = width // n_blk
    tables = tables_of(window, width // window)
    smem = pl.BlockSpec(memory_space=pltpu.SMEM)
    vmem = pl.BlockSpec(memory_space=pltpu.VMEM)
    dma = pltpu.SemaphoreType.DMA
    return pl.pallas_call(
        functools.partial(kernel, n_strip, n_blk),
        out_shape=(
            pltpu.VMEM(objects.shape, jnp.float32),
            pltpu.VMEM((2, window, share), jnp.float32),
        ),
        in_specs=[smem] * 4 + [pl.BlockSpec(memory_space=pltpu.HBM)] * 4,
        out_specs=(vmem, vmem),
        scratch_shapes=[
            pltpu.VMEM(objects.shape, jnp.float32),
            pltpu.VMEM(probe_init.shape, jnp.float32),
            pltpu.VMEM(amplitudes.shape, jnp.float32),
            pltpu.VMEM(tables.shape, jnp.bfloat16),
            pltpu.VMEM((slots, window, 128), jnp.float32),
            dma((7,)),
            pltpu.VMEM(objects.shape, jnp.float32),
            pltpu.VMEM((2 * slots, 2 * size - window, size), jnp.float32),
            pltpu.VMEM(probe_init.shape, jnp.float32),
            pltpu.VMEM(probe_init.shape, jnp.float32),
            pltpu.VMEM((n_blk, share, 128), jnp.float32),
            pltpu.VMEM((n_blk, share, 128), jnp.float32),
            pltpu.VMEM((share, 128), jnp.float32),
            pltpu.VMEM((n_strip, share, 128), jnp.float32),
            pltpu.VMEM((4, 2, 2, BORDER, size), jnp.float32),
            dma((2, RING_CHUNKS)),
            dma((n_blk,)), dma((n_blk,)),
            dma((n_strip,)), dma((n_strip,)),
            dma((4, 2)), dma((4, 2)),
        ],
        compiler_params=pltpu.CompilerParams(
            collective_id=0, has_side_effects=True, vmem_limit_bytes=60 * 1024 * 1024
        ),
    )(
        scan_rows, scan_cols, counts, offsets,
        objects, probe_init, amplitudes,
        jnp.asarray(tables),
    )


def solution(mesh):
    return jax.shard_map(
        functools.partial(shards, mesh.shape["strip"], mesh.shape["blk"]),
        mesh=mesh,
        in_specs=(
            P(None, None, "strip", "blk"),
            P(),
            P(("strip", "blk")),
            P(("strip", "blk")),
            P(("strip", "blk"), None),
            P(("strip", "blk")),
            P(),
        ),
        out_specs=(P(None, None, "strip", "blk"), P(None, None, "blk")),
        check_vma=False,
    )
```

```python
import functools

import jax
import jax.numpy as jnp
import ml_dtypes
import numpy as np
from jax import lax
from jax.experimental import pallas as pl
from jax.experimental.pallas import tpu as pltpu
from jax.sharding import PartitionSpec as P

ROUNDS = 2
BORDER = 32
RING_CHUNKS = 4
object_rate = 0.3
probe_rate = 0.5
modulus_floor = 0.25
fresnel_phase = 0.15
power_epsilon = 1e-06
MESH = pl.DeviceIdType.MESH


def two_parts(table):
    high = table.astype(ml_dtypes.bfloat16)
    low = (table - high.astype(np.float64)).astype(ml_dtypes.bfloat16)
    return high, low


def tables_of(window, modes):
    position = np.arange(window)
    angle = (position[:, None] * position[None, :] % window) * (2 * np.pi / window)
    dft = (np.cos(angle) - 1j * np.sin(angle)) / np.sqrt(window)
    frequency = np.where(position < window // 2, position, position - window)
    phase = np.exp(1j * fresnel_phase * frequency.astype(np.float64) ** 2 / window)
    fresnel = np.conj(dft) @ (phase[:, None] * dft)
    tables = []
    for matrix in (fresnel, dft, np.conj(dft), np.conj(fresnel)):
        high, low = two_parts(np.block([[matrix.real, -matrix.imag], [matrix.imag, matrix.real]]))
        pair = np.kron(np.eye(128 // window), matrix)
        tables.append(np.block([[high, high], [low, low]]))
        tables += two_parts(np.block([[pair.real, pair.imag], [-pair.imag, pair.real]]))
    return np.stack(tables).astype(ml_dtypes.bfloat16)


def halves(value):
    high = value.astype(jnp.bfloat16)
    return high, (value - high.astype(jnp.float32)).astype(jnp.bfloat16)


def product(left, right):
    return jnp.dot(left, right, preferred_element_type=jnp.float32)


def kernel(
    n_strip, n_blk,
    rows_ref, cols_ref, counts_ref, offsets_ref,
    objects_hbm, probe_hbm, amps_hbm, tables_hbm,
    out_ref, step_ref,
    objects_ref, probe_ref, amps_raw, tables, amps_ref, in_sems,
    tile, spread, probe_out, probe_in,
    shares, arrived, partial, strips, rims,
    ring_sems, share_send, share_recv, strip_send, strip_recv, rim_send, rim_recv,
):
    s, b = lax.axis_index("strip"), lax.axis_index("blk")
    window, width = probe_ref.shape[1], probe_ref.shape[2]
    modes = width // window
    slots = amps_ref.shape[0]
    size = objects_ref.shape[2]
    loads = [
        pltpu.make_async_copy(source, target, in_sems.at[i])
        for i, (source, target) in enumerate((
            (objects_hbm, objects_ref),
            (probe_hbm, probe_ref),
            (amps_hbm, amps_raw),
            *((tables_hbm.at[pl.ds(3 * i, 3)], tables.at[pl.ds(3 * i, 3)]) for i in range(4)),
        ))
    ]
    for load in loads:
        load.start()
    share = shares.shape[1]
    groups = 128 // share
    n_pairs = width // 128

    def blk_step(k):
        return lax.rem(b + k + n_blk, n_blk)

    def strip_step(k):
        return lax.rem(s + k + n_strip, n_strip)

    rims[...] = jnp.zeros_like(rims)
    barrier = pltpu.get_barrier_semaphore()
    partners = [(s, blk_step(k)) for k in range(1, n_blk)]
    partners += [(strip_step(k), b) for k in range(1, n_strip)]
    partners += [(strip_step(k), blk_step(k)) for k in (-1, 1)]
    for partner in partners:
        pl.semaphore_signal(barrier, inc=1, device_id=partner, device_id_type=MESH)

    def left_side(pairs, index):
        middles = []
        for re, im in pairs:
            stacked = jnp.concatenate(halves(jnp.concatenate([re, im], axis=0)), axis=0)
            both = product(tables[3 * index], stacked)
            total = both[: 2 * window] + both[2 * window :]
            middles.append((total[:window], total[window:]))
        return middles

    def right_side(pairs, index):
        rows = pairs[0][0].shape[0]
        blocks = []
        for re, im in pairs:
            for start in range(0, width, 128):
                blocks.append(jnp.concatenate([re[:, start : start + 128], im[:, start : start + 128]], axis=1))
        high, low = halves(jnp.concatenate(blocks, axis=0))
        count = high.shape[0]
        both = product(jnp.concatenate([high, low], axis=0), tables[3 * index + 1])
        total = both[:count] + both[count:] + product(high, tables[3 * index + 2])
        results = []
        for j in range(len(pairs)):
            mine = [total[(j * n_pairs + p) * rows : (j * n_pairs + p + 1) * rows] for p in range(n_pairs)]
            results.append(tuple(
                jnp.concatenate([x[:, part * 128 : (part + 1) * 128] for x in mine], axis=1) for part in range(2)
            ))
        return results

    def transform(pairs, index):
        return [right_side(left_side([pair], index), index)[0] for pair in pairs]

    def times(x, y):
        return x[0] * y[0] - x[1] * y[1], x[0] * y[1] + x[1] * y[0]

    def conj_times(x, y):
        return x[0] * y[0] + x[1] * y[1], x[0] * y[1] - x[1] * y[0]

    lane = lax.broadcasted_iota(jnp.int32, (window, 128), 1)

    def over_modes(value):
        total = value[:, :128]
        for start in range(128, width, 128):
            total = total + value[:, start : start + 128]
        return total + pltpu.roll(total, window, 1)

    def widened(value):
        return jnp.concatenate([value] * (width // 128), axis=1)

    def window_of(source, part, layer, j):
        rows = source[part, layer, pl.ds(rows_ref[j], window), :]
        rows = pltpu.roll(rows, lax.rem(size - cols_ref[j], size), 1)
        return widened(jnp.where(lane < window, rows, pltpu.roll(rows, window, 1)))

    def total_of(value):
        return jnp.sum(jnp.sum(value, axis=0, keepdims=True), axis=1, keepdims=True)

    spread[...] = jnp.zeros_like(spread)

    def placed(buffer, value, j):
        spread[buffer, pl.ds(size - window, window), :] = jnp.where(lane < window, value, 0.0)
        rows = spread[buffer, pl.ds(size - window - rows_ref[j], size), :]
        return pltpu.roll(rows, cols_ref[j], 1)

    def unfold_amps():
        first = lax.broadcasted_iota(jnp.int32, (slots, 128), 1) < window
        for i in range(window * window // 128):
            pair = amps_raw[:, pl.ds(128 * i, 128)]
            turned = pltpu.roll(pair, window, 1)
            amps_ref[:, 2 * i, :] = jnp.where(first, pair, turned)
            amps_ref[:, 2 * i + 1, :] = jnp.where(first, turned, pair)

    rim_rows = (pl.ds(0, BORDER), pl.ds(size - BORDER, BORDER))
    rim_plan = (
        (0, -1, 0, s > 0, s < n_strip - 1),
        (0, -1, -1, (s > 0) & (b > 0), (s < n_strip - 1) & (b < n_blk - 1)),
        (1, 1, 0, s < n_strip - 1, s > 0),
        (1, 1, 1, (s < n_strip - 1) & (b < n_blk - 1), (s > 0) & (b > 0)),
    )

    def rim_copy(layer, kind):
        edge, ds, db, _, _ = rim_plan[kind]
        return pltpu.make_async_remote_copy(
            src_ref=tile.at[:, layer, rim_rows[edge], :],
            dst_ref=rims.at[kind, layer],
            send_sem=rim_send.at[kind, layer],
            recv_sem=rim_recv.at[kind, layer],
            device_id=(strip_step(ds), blk_step(db)),
            device_id_type=MESH,
        )

    def send_rims(layer):
        for kind in range(4):
            @pl.when(rim_plan[kind][3])
            def _():
                rim_copy(layer, kind).start()

    chunk = window // RING_CHUNKS
    chunks = [slice(i * chunk, (i + 1) * chunk) for i in range(RING_CHUNKS)]

    def ring_copy(i):
        rows = pl.ds(i * chunk, chunk)
        return pltpu.make_async_remote_copy(
            src_ref=probe_out.at[:, rows, :], dst_ref=probe_in.at[:, rows, :],
            send_sem=ring_sems.at[0, i], recv_sem=ring_sems.at[1, i],
            device_id=(s, blk_step(1)), device_id_type=MESH,
        )

    ring = [ring_copy(i) for i in range(RING_CHUNKS)]

    def cut(pair, rows):
        return pair[0][rows], pair[1][rows]

    def joined(pieces):
        return tuple(jnp.concatenate([piece[part] for piece in pieces], axis=0) for part in range(2))

    for round_index in range(ROUNDS):
        last = round_index == ROUNDS - 1
        source = objects_ref if round_index == 0 else tile
        probe_src = probe_ref if round_index == 0 else probe_in
        if round_index == 0:
            loads[0].wait()
        powers = []
        for layer in range(2):
            squares = source[0, layer] ** 2 + source[1, layer] ** 2
            powers.append(total_of(squares) / (size * size) + power_epsilon)
        objects = [
            [(window_of(source, 0, layer, j), window_of(source, 1, layer, j)) for j in range(slots)]
            for layer in range(2)
        ]
        if round_index > 0:
            middles = []
            for i in range(RING_CHUNKS):
                ring[i].wait_recv()
                piece = (probe_in[0, pl.ds(i * chunk, chunk)], probe_in[1, pl.ds(i * chunk, chunk)])
                middles.append(right_side([times(piece, cut(objects[0][j], chunks[i])) for j in range(slots)], 0))
            arrivals = left_side([joined([piece[j] for piece in middles]) for j in range(slots)], 0)
            for copy in ring:
                copy.wait_send()
        else:
            loads[1].wait()
            loads[3].wait()
        probe = (probe_src[0], probe_src[1])
        probe_power = total_of(probe[0] ** 2 + probe[1] ** 2) / (window * window) + power_epsilon
        if round_index == 0:
            arrivals = transform([times(probe, objects[0][j]) for j in range(slots)], 0)
        if round_index == 0:
            loads[2].wait()
            unfold_amps()
            loads[4].wait()
        far = transform([times(arrivals[j], objects[1][j]) for j in range(slots)], 1)
        changes = []
        for j in range(slots):
            weight = jnp.where(counts_ref[0] > j, 1.0, 0.0)
            modulus = jnp.sqrt(over_modes(far[j][0] ** 2 + far[j][1] ** 2))
            factor = widened((amps_ref[j] / jnp.maximum(modulus, modulus_floor) - 1.0) * weight)
            changes.append((far[j][0] * factor, far[j][1] * factor))
        if round_index == 0:
            loads[5].wait()
        exits = transform(changes, 2)

        if round_index == 0:
            loads[6].wait()
        returns = [conj_times(objects[1][j], exits[j]) for j in range(slots)]
        probe_gain = probe_rate / (powers[0] * powers[1] * slots)

        def moved_probe(pieces, rows):
            terms = [conj_times(cut(objects[0][j], rows), pieces[j]) for j in range(slots)]
            moved = []
            for part in range(2):
                total = terms[0][part]
                for j in range(1, slots):
                    total = total + terms[j][part]
                moved.append(probe[part][rows] + probe_gain * total)
            return moved

        if not last:
            middles = left_side(returns, 3)
            pieces = []
            for i in range(RING_CHUNKS):
                pieces.append(right_side([cut(middle, chunks[i]) for middle in middles], 3))
                for part, value in enumerate(moved_probe(pieces[i], chunks[i])):
                    probe_out[part, pl.ds(i * chunk, chunk)] = value
                if round_index == 0 and i == 0:
                    pl.semaphore_wait(barrier, len(partners))
                ring[i].start()
            entries = [joined([piece[j] for piece in pieces]) for j in range(slots)]
        else:
            entries = transform(returns, 3)
            moved = moved_probe(entries, slice(0, window))
            stacked = jnp.concatenate([moved[0] - probe_ref[0], moved[1] - probe_ref[1]], axis=0)
            group_of = lax.broadcasted_iota(jnp.int32, (share, 128), 1) // share
            for h in range(width // 128):
                for i in range(groups):
                    packed = None
                    for k in range(groups):
                        block = stacked[k * share : (k + 1) * share, h * 128 : (h + 1) * 128]
                        if k != i:
                            block = pltpu.roll(block, (k - i) % groups * share, 1)
                        packed = block if packed is None else jnp.where(group_of == k, block, packed)
                    shares[h * groups + i] = packed
            share_copies = []
            for k in range(1, n_blk):
                share_copies.append(
                    pltpu.make_async_remote_copy(
                        src_ref=shares.at[blk_step(k)], dst_ref=arrived.at[k],
                        send_sem=share_send.at[k], recv_sem=share_recv.at[k],
                        device_id=(s, blk_step(k)), device_id_type=MESH,
                    )
                )
                share_copies[-1].start()

        second_gain = object_rate / (probe_power * powers[0] * slots)
        for part in range(2):
            total = source[part, 1]
            for j in range(slots):
                update = over_modes(conj_times(arrivals[j], exits[j])[part]) * second_gain
                total = total + placed(2 * j + part, update, j)
            tile[part, 1] = total
        if last:
            send_rims(1)
        first_gain = object_rate / (probe_power * slots)
        for part in range(2):
            total = source[part, 0]
            for j in range(slots):
                update = over_modes(conj_times(probe, entries[j])[part]) * first_gain
                total = total + placed(2 * j + part, update, j)
            tile[part, 0] = total
        if last:
            send_rims(0)

    own = shares[b]
    for k in range(1, n_blk):
        share_copies[k - 1].wait_recv()
        own = own + arrived[k]
    partial[...] = own
    strip_copies = []
    for k in range(1, n_strip):
        strip_copies.append(
            pltpu.make_async_remote_copy(
                src_ref=partial, dst_ref=strips.at[k],
                send_sem=strip_send.at[k], recv_sem=strip_recv.at[k],
                device_id=(strip_step(k), b), device_id_type=MESH,
            )
        )
        strip_copies[-1].start()

    for part in range(2):
        for layer in range(2):
            out_ref[part, layer, pl.ds(BORDER, size - 2 * BORDER), :] = tile[
                part, layer, pl.ds(BORDER, size - 2 * BORDER), :
            ]
    for layer in (1, 0):
        for kind in range(4):
            @pl.when(rim_plan[kind][4])
            def _():
                rim_copy(layer, kind).wait_recv()
    column = lax.broadcasted_iota(jnp.int32, (BORDER, size), 1)
    down = offsets_ref[s]
    up = offsets_ref[jnp.maximum(s - 1, 0)]
    for layer in range(2):
        for part in range(2):
            partner = pltpu.roll(
                jnp.where(column >= down, rims[0, layer, part], rims[1, layer, part]),
                lax.rem(size - down, size), 1,
            )
            valid = (s < n_strip - 1) & ((b < n_blk - 1) | (column + down < size))
            mine = tile[part, layer, rim_rows[1], :]
            out_ref[part, layer, rim_rows[1], :] = jnp.where(valid, 0.5 * (mine + partner), mine)
            partner = pltpu.roll(
                jnp.where(column < size - up, rims[2, layer, part], rims[3, layer, part]), up, 1
            )
            valid = (s > 0) & ((b > 0) | (column >= up))
            mine = tile[part, layer, rim_rows[0], :]
            out_ref[part, layer, rim_rows[0], :] = jnp.where(valid, 0.5 * (mine + partner), mine)

    total = partial[...]
    for k in range(1, n_strip):
        strip_copies[k - 1].wait_recv()
        total = total + strips[k]
    total = total / (n_strip * n_blk)
    for k in range(groups):
        block = total if k == 0 else pltpu.roll(total, (groups - k) * share, 1)
        part, row = divmod(k * share, window)
        step_ref[part, pl.ds(row, share), :] = block[:, :share]

    for copy in share_copies + strip_copies:
        copy.wait_send()
    for layer in range(2):
        for kind in range(4):
            @pl.when(rim_plan[kind][3])
            def _():
                rim_copy(layer, kind).wait_send()


def shards(n_strip, n_blk, objects, probe_init, scan_rows, scan_cols, amplitudes, counts, offsets):
    window, width = probe_init.shape[1], probe_init.shape[2]
    slots = scan_rows.shape[0]
    size = objects.shape[2]
    share = width // n_blk
    tables = tables_of(window, width // window)
    smem = pl.BlockSpec(memory_space=pltpu.SMEM)
    vmem = pl.BlockSpec(memory_space=pltpu.VMEM)
    dma = pltpu.SemaphoreType.DMA
    return pl.pallas_call(
        functools.partial(kernel, n_strip, n_blk),
        out_shape=(
            pltpu.VMEM(objects.shape, jnp.float32),
            pltpu.VMEM((2, window, share), jnp.float32),
        ),
        in_specs=[smem] * 4 + [pl.BlockSpec(memory_space=pltpu.HBM)] * 4,
        out_specs=(vmem, vmem),
        scratch_shapes=[
            pltpu.VMEM(objects.shape, jnp.float32),
            pltpu.VMEM(probe_init.shape, jnp.float32),
            pltpu.VMEM(amplitudes.shape, jnp.float32),
            pltpu.VMEM(tables.shape, jnp.bfloat16),
            pltpu.VMEM((slots, window, 128), jnp.float32),
            dma((7,)),
            pltpu.VMEM(objects.shape, jnp.float32),
            pltpu.VMEM((2 * slots, 2 * size - window, size), jnp.float32),
            pltpu.VMEM(probe_init.shape, jnp.float32),
            pltpu.VMEM(probe_init.shape, jnp.float32),
            pltpu.VMEM((n_blk, share, 128), jnp.float32),
            pltpu.VMEM((n_blk, share, 128), jnp.float32),
            pltpu.VMEM((share, 128), jnp.float32),
            pltpu.VMEM((n_strip, share, 128), jnp.float32),
            pltpu.VMEM((4, 2, 2, BORDER, size), jnp.float32),
            dma((2, RING_CHUNKS)),
            dma((n_blk,)), dma((n_blk,)),
            dma((n_strip,)), dma((n_strip,)),
            dma((4, 2)), dma((4, 2)),
        ],
        compiler_params=pltpu.CompilerParams(
            collective_id=0, has_side_effects=True, vmem_limit_bytes=60 * 1024 * 1024
        ),
    )(
        scan_rows, scan_cols, counts, offsets,
        objects, probe_init, amplitudes,
        jnp.asarray(tables),
    )


def solution(mesh):
    return jax.shard_map(
        functools.partial(shards, mesh.shape["strip"], mesh.shape["blk"]),
        mesh=mesh,
        in_specs=(
            P(None, None, "strip", "blk"),
            P(),
            P(("strip", "blk")),
            P(("strip", "blk")),
            P(("strip", "blk"), None),
            P(("strip", "blk")),
            P(),
        ),
        out_specs=(P(None, None, "strip", "blk"), P(None, None, "blk")),
        check_vma=False,
    )
```
